128 devices in a mesh: dp: 16 (over z, x_hi, core), tensor: 8 (over x_lo, y).
Axes of the slice: x: 4 (x_hi: 2, x_lo: 2; x = x_hi * 2 + x_lo), y: 4, z: 4, core: 2. Of those that a mesh axis runs over, the one named last changes fastest.
Arguments:
- queries: bfloat16 [2048, 8192], P('dp', 'tensor'), may hold values from -130 to 130
- new_key: bfloat16 [2048, 1024], P('dp', 'tensor'), may hold values from -5 to 5
- new_value: bfloat16 [2048, 1024], P('dp', 'tensor'), may hold values from -5 to 5
- cache_keys: bfloat16 [2048, 8, 128, 128], P('dp', 'tensor'), may hold values from -5 to 5
- cache_values: bfloat16 [2048, 8, 128, 128], P('dp', 'tensor'), may hold values from -5 to 5
- lengths: int32 [2048], P('dp'), may hold values from 2 to 128, as said below
- prefix_keys: bfloat16 [32, 8, 2048, 128], P('dp', 'tensor'), may hold values from -5 to 5
- prefix_values: bfloat16 [32, 8, 2048, 128], P('dp', 'tensor'), may hold values from -5 to 5
- prompt_ids: int32 [2048], P('dp'), may hold values from 0 to 31, as said below
- cluster_ids: int32 [2048], P('dp'), may hold values from 0 to 15
- out_weight: bfloat16 [8192, 8192], P('tensor', 'dp'), may hold values from -0.25 to 0.25
- residual: bfloat16 [2048, 8192], P('tensor', 'dp'), may hold values from -4 to 4
- norm_gain: bfloat16 [8192], P('dp'), may hold values from 0.099609375 to 1.8984375
- up_weight: bfloat16 [8192, 4096], P('dp'), may hold values from -0.09375 to 0.09375
- head_weight: bfloat16 [4096], replicated, may hold values from -0.09375 to 0.09375
Outputs:
- hidden: bfloat16 [2048, 8192], P('tensor', 'dp')
- scores: float32 [2048], P('tensor')
- votes: float32 [32, 16], replicated
The draws below stay inside these ranges and needn't reach their ends.
Inputs may be any that keep to these rules, and one draw needn't show every extreme that they name: `lengths`: live slots of a row; some row in every draw has all 128. `prompt_ids`: rows k * 128 to (k + 1) * 128 - 1 belong to prompts k * 2 to (k + 1) * 2 - 1.
All inputs are finite; a program needn't handle non-finite values.
Results may differ from the reference program's by a relative error of at most 0.015.
Values may be sent and summed in bfloat16 or wider, within the bound.
No kernel may reach another device: no remote copies, remote signals or barrier semaphores. Data moves between devices by JAX's collectives and lax.ppermute only.
A program may use at most 128 MiB of HBM per device.

```python
import math
import jax
import jax.numpy as jnp
from jax import lax

D = 8192
HQ = 64
KVH = 8
HD = 128
DV = 4096
PREFIX = 2048
GEN = 128
PROMPTS_DEV = 2
CLUSTERS = 16
ROWS_DEV = 128
ROWS = 2048
PROMPTS = 32
N_DP = 16


def shared_keys(key):
    new_keys = jnp.clip(jax.random.normal(jax.random.fold_in(key, 101), (ROWS, KVH * HD), jnp.float32), -5.0, 5.0)
    lead_keys = jnp.clip(jax.random.normal(jax.random.fold_in(key, 102), (ROWS, KVH, HD), jnp.float32), -5.0, 5.0)
    return (new_keys, lead_keys)


def draw_new_key(key, part):
    new_keys, lead_keys = shared_keys(key)
    return new_keys.astype(jnp.bfloat16)


def draw_cache_keys(key, part):
    new_keys, lead_keys = shared_keys(key)
    other_key = jax.random.fold_in(key, 3)
    others = jnp.clip(jax.random.normal(other_key, (ROWS, KVH, GEN - 1, HD), jnp.float32), -5.0, 5.0)
    second = others[:, :, 0, :]
    cache = jnp.concatenate([lead_keys[:, :, None, :], second[:, :, None, :], others[:, :, 1:, :]], axis=2)
    return cache.astype(jnp.bfloat16)


def draw_queries(key, part):
    new_keys, lead_keys = shared_keys(key)
    noise_key = jax.random.fold_in(key, 5)
    noise = jnp.clip(jax.random.normal(noise_key, (ROWS, KVH, HQ // KVH, HD), jnp.float32), -5.0, 5.0)
    base = noise + 0.5 * new_keys.reshape(ROWS, KVH, 1, HD)
    return base.reshape(ROWS, HQ * HD).astype(jnp.bfloat16)


def draw_lengths(key, part):
    key = jax.random.fold_in(key, 7)
    values = jax.random.randint(jax.random.fold_in(key, 1), (ROWS,), 2, GEN + 1, jnp.int32)
    longest = jax.random.randint(jax.random.fold_in(key, 2), (), 0, ROWS, jnp.int32)
    return values.at[longest].set(GEN).astype(jnp.int32)


def draw_prompt_ids(key, part):
    key = jax.random.fold_in(key, 9)
    local = jax.random.randint(key, (ROWS,), 0, PROMPTS_DEV, jnp.int32)
    return (local + jnp.arange(ROWS, dtype=jnp.int32) // ROWS_DEV * PROMPTS_DEV).astype(jnp.int32)


def draw_residual(key, part):
    key = jax.random.fold_in(key, 11)
    column_pos = jnp.arange(D, dtype=jnp.float32) / D
    column_scale = jnp.exp(jnp.log(3.0) * column_pos) * jax.random.uniform(jax.random.fold_in(key, 1), (D,), jnp.float32, 0.6, 1.4) / 1.7
    row_scale = jnp.exp(jax.random.uniform(jax.random.fold_in(key, 2), (ROWS,), jnp.float32, jnp.log(0.3), jnp.log(3.0)))
    base = jnp.clip(jax.random.normal(jax.random.fold_in(key, 3), (ROWS, D), jnp.float32), -4.0, 4.0)
    return (base * row_scale[:, None] * column_scale[None, :] * 0.125).astype(jnp.bfloat16)


def set_ends(drawn, key, least, largest):
    longest = drawn.shape.index(max(drawn.shape))
    spots = []
    for shift in (0, 1):
        where = [jax.random.randint(jax.random.fold_in(key, axis), (), 0, length) for axis, length in enumerate(drawn.shape)]
        where[longest] = (where[longest] + shift) % drawn.shape[longest]
        spots.append(tuple(where))
    return drawn.at[spots[0]].set(least).at[spots[1]].set(largest)


def spiked(values, rng, source, target, parts, factor):
    def block_of(position):
        return (jnp.arange(values.shape[position]) // (values.shape[position] // parts)).reshape((-1,) + (1,) * (values.ndim - 1 - position))

    one_side = jax.random.permutation(rng, parts)[block_of(target)]
    second = (block_of(target) + parts // 2) % parts
    return jnp.where((block_of(source) == one_side) | (block_of(source) == second), factor * values, values)


def block_scale(rng, dims, cuts, least, high):
    loudness = 1.0
    for axis_at, shards_of in cuts:
        steps = jax.random.uniform(jax.random.fold_in(jax.random.fold_in(rng, 6), axis_at), (shards_of,), jnp.float32, least / len(cuts), high / len(cuts))
        loudness = loudness * jnp.repeat(jnp.exp(steps), dims[axis_at] // shards_of).reshape((-1,) + (1,) * (len(dims) - 1 - axis_at))
    return loudness


def gaussian(stream_key, extent, width, bound, cuts=(), held_as=jnp.bfloat16):
    factor_of = block_scale(stream_key, extent, cuts, -0.22, 0.18) if cuts else 1.0
    drawn = jax.random.normal(stream_key, extent, jnp.float32) * width * factor_of
    return jnp.minimum(jnp.maximum(drawn, -bound), bound).astype(held_as)


def noise_with(key, dims, width, bound, pieces, heavy, held_as=jnp.bfloat16):
    drawn = width * jax.random.normal(key, dims, jnp.float32)
    if pieces:
        drawn = drawn * block_scale(key, dims, pieces, -0.22, 0.18)
    return jnp.clip(spiked(drawn, jax.random.fold_in(key, 3), *heavy), -bound, bound).astype(held_as)


def setup_inputs(seed: int = 0) -> dict:
    arg_keys = jax.random.split(jax.random.key(seed), 16)
    queries = draw_queries(jax.random.fold_in(arg_keys[15], 71), 0)
    new_key = draw_new_key(jax.random.fold_in(arg_keys[15], 71), 0)
    new_value = gaussian(arg_keys[2], (ROWS, KVH * HD), 1.0, 5.0, ((0, 16), (1, 8)))
    cache_keys = draw_cache_keys(jax.random.fold_in(arg_keys[15], 71), 0)
    cache_values = gaussian(arg_keys[4], (ROWS, KVH, GEN, HD), 1.0, 5.0, ((0, 16), (1, 8)))
    lengths = draw_lengths(jax.random.fold_in(arg_keys[15], 71), 0)
    prefix_keys = gaussian(arg_keys[6], (PROMPTS, KVH, PREFIX, HD), 1.0, 5.0, ((0, 16), (1, 8)))
    prefix_values = gaussian(arg_keys[7], (PROMPTS, KVH, PREFIX, HD), 1.0, 5.0, ((0, 16), (1, 8)))
    prompt_ids = draw_prompt_ids(jax.random.fold_in(arg_keys[15], 71), 0)
    cluster_ids = set_ends(jax.random.randint(arg_keys[9], (ROWS,), 0, CLUSTERS), jax.random.fold_in(arg_keys[9], 1), 0, CLUSTERS - 1).astype(jnp.int32)
    out_weight = gaussian(arg_keys[10], (HQ * HD, D), (HQ * HD // 16) ** -0.5, 0.25, ((0, 8), (1, 16)))
    residual = draw_residual(jax.random.fold_in(arg_keys[15], 71), 0)
    norm_gain = jnp.clip(1.0 + 0.18 * jax.random.normal(arg_keys[12], (D,), jnp.float32), 0.099609375, 1.8984375).astype(jnp.bfloat16)
    up_weight = noise_with(arg_keys[13], (D, DV), D ** -0.5, 0.09375, ((0, 16),), (0, 1, 16, 2.0))
    head_weight = gaussian(arg_keys[14], (DV,), DV ** -0.5, 0.09375)
    return dict(queries=queries, new_key=new_key, new_value=new_value, cache_keys=cache_keys, cache_values=cache_values, lengths=lengths, prefix_keys=prefix_keys, prefix_values=prefix_values, prompt_ids=prompt_ids, cluster_ids=cluster_ids, out_weight=out_weight, residual=residual, norm_gain=norm_gain, up_weight=up_weight, head_weight=head_weight)


eps = 1e-05

def attend(queries, new_key, new_value, cache_keys, cache_values, lengths, prefix_keys, prefix_values, local_prompt):
    rows_blk = queries.shape[0]
    kv_heads = cache_keys.shape[1]
    head_dim = cache_keys.shape[3]
    groups = queries.shape[1] // (kv_heads * head_dim)
    prompts_blk = prefix_keys.shape[0]
    gen_len = cache_keys.shape[2]
    score_scale = 1.0 / math.sqrt(head_dim)
    grouped = queries.reshape(rows_blk, kv_heads, groups, head_dim).astype(jnp.float32)
    pre_scores = jnp.einsum('rkgd,pkjd->rkgpj', grouped, prefix_keys.astype(jnp.float32)) * score_scale
    pre_ok = (local_prompt[:, None] == jnp.arange(prompts_blk, dtype=jnp.int32)[None, :])[:, None, None, :, None]
    gen_scores = jnp.einsum('rkgd,rkjd->rkgj', grouped, cache_keys.astype(jnp.float32)) * score_scale
    gen_ok = (jnp.arange(gen_len, dtype=jnp.int32)[None, :] < lengths[:, None])[:, None, None, :]
    own_key = new_key.reshape(rows_blk, kv_heads, head_dim).astype(jnp.float32)
    own_scores = jnp.einsum('rkgd,rkd->rkg', grouped, own_key) * score_scale
    pre_scores = jnp.where(pre_ok, pre_scores, -1e+30)
    gen_scores = jnp.where(gen_ok, gen_scores, -1e+30)
    row_top = jnp.maximum(jnp.maximum(lax.optimization_barrier(jnp.max(pre_scores, axis=(3, 4))), lax.optimization_barrier(jnp.max(gen_scores, axis=3))), own_scores)
    pre_exp = jnp.exp(pre_scores - row_top[..., None, None])
    gen_exp = jnp.exp(gen_scores - row_top[..., None])
    own_exp = jnp.exp(own_scores - row_top)
    denominator = lax.optimization_barrier(jnp.sum(pre_exp, axis=(3, 4))) + lax.optimization_barrier(jnp.sum(gen_exp, axis=3)) + own_exp
    pre_w = (pre_exp / denominator[..., None, None]).astype(jnp.bfloat16)
    gen_w = (gen_exp / denominator[..., None]).astype(jnp.bfloat16)
    own_w = (own_exp / denominator).astype(jnp.bfloat16)
    own_val = new_value.reshape(rows_blk, kv_heads, head_dim).astype(jnp.float32)
    result = jnp.einsum('rkgpj,pkjd->rkgd', pre_w.astype(jnp.float32), prefix_values.astype(jnp.float32))
    result = result + jnp.einsum('rkgj,rkjd->rkgd', gen_w.astype(jnp.float32), cache_values.astype(jnp.float32))
    result = result + own_w.astype(jnp.float32)[..., None] * own_val[:, :, None, :]
    return result.reshape(rows_blk, kv_heads * groups * head_dim).astype(jnp.bfloat16)

def reference(queries, new_key, new_value, cache_keys, cache_values, lengths, prefix_keys, prefix_values, prompt_ids, cluster_ids, out_weight, residual, norm_gain, up_weight, head_weight):

    def one_block(block):
        row_lo = (block * ROWS_DEV).astype(jnp.int32)
        pro_lo = (block * PROMPTS_DEV).astype(jnp.int32)

        def rows_of(array):
            return lax.dynamic_slice_in_dim(array, row_lo, ROWS_DEV, 0)
        local_prompt = rows_of(prompt_ids) - pro_lo
        return attend(rows_of(queries), rows_of(new_key), rows_of(new_value), rows_of(cache_keys), rows_of(cache_values), rows_of(lengths), lax.dynamic_slice_in_dim(prefix_keys, pro_lo, PROMPTS_DEV, 0), lax.dynamic_slice_in_dim(prefix_values, pro_lo, PROMPTS_DEV, 0), local_prompt)
    attended = lax.map(one_block, jnp.arange(N_DP, dtype=jnp.int32)).reshape(ROWS, HQ * HD)
    mixed_out = jnp.dot(attended, out_weight, preferred_element_type=jnp.float32)
    hidden = (residual.astype(jnp.float32) + mixed_out).astype(jnp.bfloat16)
    widened = hidden.astype(jnp.float32)
    squares = lax.optimization_barrier(jnp.sum(widened * widened, axis=1))
    normed = (widened * lax.rsqrt(squares / D + eps)[:, None] * norm_gain.astype(jnp.float32)[None, :]).astype(jnp.bfloat16)
    verifier_up = jnp.dot(normed, up_weight, preferred_element_type=jnp.float32)
    scores = lax.optimization_barrier(jnp.sum(jax.nn.silu(verifier_up) * head_weight.astype(jnp.float32)[None, :], axis=1))
    pair_ids = prompt_ids * CLUSTERS + cluster_ids
    vote_sums = jax.ops.segment_sum(scores, pair_ids, num_segments=PROMPTS * CLUSTERS)
    return (hidden, scores, vote_sums.reshape(PROMPTS, CLUSTERS))
```

```python
import math

import jax
import jax.numpy as jnp
from jax import lax
from jax.experimental import pallas as pl
from jax.experimental.pallas import tpu as pltpu
from jax.sharding import Mesh, PartitionSpec as P

D = 8192
CLUSTERS = 16
PROMPTS_DEV = 2
eps = 1e-05
AXES = ("z", "xh", "c", "xl", "yh", "yl")
DP = ("z", "xh", "c")
TP = ("xl", "yh", "yl")
BF = jnp.bfloat16
F32 = jnp.float32


def attend(
    queries,
    new_key,
    new_value,
    cache_keys,
    cache_values,
    lengths,
    prefix_keys,
    prefix_values,
    local_prompt,
):
    rows_blk = queries.shape[0]
    kv_heads = cache_keys.shape[1]
    head_dim = cache_keys.shape[3]
    groups = queries.shape[1] // (kv_heads * head_dim)
    prompts_blk = prefix_keys.shape[0]
    gen_len = cache_keys.shape[2]
    score_scale = 1.0 / math.sqrt(head_dim)
    grouped = queries.reshape(rows_blk, kv_heads, groups, head_dim)
    pre_scores = (
        jnp.einsum("rkgd,pkjd->rkgpj", grouped, prefix_keys, preferred_element_type=jnp.float32)
        * score_scale
    )
    pre_ok = (local_prompt[:, None] == jnp.arange(prompts_blk, dtype=jnp.int32)[None, :])[
        :, None, None, :, None
    ]
    gen_scores = (
        jnp.einsum("rkgd,rkjd->rkgj", grouped, cache_keys, preferred_element_type=jnp.float32)
        * score_scale
    )
    gen_ok = (jnp.arange(gen_len, dtype=jnp.int32)[None, :] < lengths[:, None])[:, None, None, :]
    own_key = new_key.reshape(rows_blk, kv_heads, head_dim)
    own_scores = (
        jnp.einsum("rkgd,rkd->rkg", grouped, own_key, preferred_element_type=jnp.float32)
        * score_scale
    )
    pre_scores = jnp.where(pre_ok, pre_scores, -1e30)
    gen_scores = jnp.where(gen_ok, gen_scores, -1e30)
    row_top = jnp.maximum(
        jnp.maximum(jnp.max(pre_scores, axis=(3, 4)), jnp.max(gen_scores, axis=3)), own_scores
    )
    pre_exp = jnp.exp(pre_scores - row_top[..., None, None])
    gen_exp = jnp.exp(gen_scores - row_top[..., None])
    own_exp = jnp.exp(own_scores - row_top)
    denominator = jnp.sum(pre_exp, axis=(3, 4)) + jnp.sum(gen_exp, axis=3) + own_exp
    pre_w = (pre_exp / denominator[..., None, None]).astype(jnp.bfloat16)
    gen_w = (gen_exp / denominator[..., None]).astype(jnp.bfloat16)
    own_w = (own_exp / denominator).astype(jnp.bfloat16)
    own_val = new_value.reshape(rows_blk, kv_heads, head_dim).astype(jnp.float32)
    result = jnp.einsum(
        "rkgpj,pkjd->rkgd", pre_w, prefix_values, preferred_element_type=jnp.float32
    )
    result = result + jnp.einsum(
        "rkgj,rkjd->rkgd", gen_w, cache_values, preferred_element_type=jnp.float32
    )
    result = result + own_w.astype(jnp.float32)[..., None] * own_val[:, :, None, :]
    return result.reshape(rows_blk, kv_heads * groups * head_dim).astype(jnp.bfloat16)


def swap(x, axis):
    return lax.ppermute(x, axis, [(0, 1), (1, 0)])


def shift(x, by):
    return lax.ppermute(x, "z", [(i, (i + by) % 4) for i in range(4)])


def proj_kernel(z_ref, here, before, after, far_a, far_b, w00, w01, w10, w11, out_ref):
    step = pl.program_id(0)

    def work(a, rows):
        own, par = a[:, :1024], a[:, 1024:]
        for j, (wo, wp) in enumerate(((w00, w10), (w01, w11))):
            acc = jnp.dot(own, wo[...], preferred_element_type=F32)
            acc = acc + jnp.dot(par, wp[...], preferred_element_type=F32)
            out_ref[0, rows, j * 512 : (j + 1) * 512] = acc.astype(BF)

    full = slice(0, 128)

    @pl.when(step == 0)
    def _():
        work(here[...], full)

    @pl.when(step == 1)
    def _():
        work(before[...], full)

    @pl.when(step == 2)
    def _():
        work(jnp.concatenate([far_a[...], far_b[...]], axis=0), full)

    @pl.when(step == 3)
    def _():
        work(after[...], full)


def project(here, before, after, far_a, far_b, w00, w01, w10, w11):
    z = lax.axis_index("z").astype(jnp.int32).reshape(1)
    whole = lambda a: pl.BlockSpec(a.shape, lambda s, z_ref: (0,) * a.ndim)
    ins = (here, before, after, far_a, far_b, w00, w01, w10, w11)
    return pl.pallas_call(
        proj_kernel,
        out_shape=jax.ShapeDtypeStruct((4, 128, 1024), BF),
        grid_spec=pltpu.PrefetchScalarGridSpec(
            num_scalar_prefetch=1,
            grid=(4,),
            in_specs=[whole(a) for a in ins],
            out_specs=pl.BlockSpec((1, 128, 1024), lambda s, z_ref: ((z_ref[0] + 4 - s) % 4, 0, 0)),
        ),
        compiler_params=pltpu.CompilerParams(vmem_limit_bytes=40 * 1024 * 1024),
        cost_estimate=pl.CostEstimate(
            flops=2 * 512 * 2048 * 1024, bytes_accessed=7 * 1024 * 1024, transcendentals=0
        ),
    )(z, *ins)


def body(
    queries,
    new_key,
    new_value,
    cache_keys,
    cache_values,
    lengths,
    prefix_keys,
    prefix_values,
    prompt_ids,
    cluster_ids,
    out_weight,
    residual,
    norm_gain,
    up_weight,
    head_weight,
):
    c = lax.axis_index("c")
    xh = lax.axis_index("xh")
    yl = lax.axis_index("yl")
    t = lax.axis_index(TP)
    dp_index = lax.axis_index(DP)
    local_prompt = prompt_ids - dp_index * PROMPTS_DEV

    w00 = out_weight
    w10 = swap(out_weight, "yl")
    w01 = swap(w00, "c")
    w11 = swap(w10, "c")
    up_par = swap(up_weight, "c")
    res_mine = lax.dynamic_slice_in_dim(residual, c * 128, 128, 0)
    res_send = lax.dynamic_slice_in_dim(residual, (1 - c) * 128, 128, 0)
    extra = swap(
        jnp.concatenate([res_send, jnp.broadcast_to(norm_gain[None, :], (16, 512))], axis=0), "c"
    )
    res_par, gain_par = extra[:128], extra[128]

    attended = attend(
        queries,
        new_key,
        new_value,
        cache_keys,
        cache_values,
        lengths,
        prefix_keys,
        prefix_values,
        local_prompt,
    )

    first = lax.ppermute(attended, ("xh", "yl"), [(0, 2), (3, 1), (1, 0), (2, 3)])
    second = lax.ppermute(attended, ("xh", "yl"), [(1, 2), (2, 1)])
    diagonal = xh == yl
    here = jnp.concatenate(
        [jnp.where(diagonal, attended, first), jnp.where(diagonal, first, second)], axis=1
    )
    before = shift(here, 1)
    after = shift(here, -1)
    far_a = shift(before[:64], 1)
    far_b = shift(after[64:], -1)
    partial = project(here, before, after, far_a, far_b, w00, w01, w10, w11)
    parts = lax.all_to_all(partial, ("xl", "yh"), 0, 0, tiled=True)
    mixed = jnp.sum(parts.astype(F32), axis=0)
    hid_mine = (res_mine.astype(F32) + mixed[:, :512]).astype(BF)
    hid_par = (res_par.astype(F32) + mixed[:, 512:]).astype(BF)
    hid_back = swap(hid_par, "c")
    hidden = jnp.where(
        c == 0,
        jnp.concatenate([hid_mine, hid_back], axis=0),
        jnp.concatenate([hid_back, hid_mine], axis=0),
    )

    wide_mine, wide_par = hid_mine.astype(F32), hid_par.astype(F32)
    squares = jnp.sum(wide_mine * wide_mine, axis=1) + jnp.sum(wide_par * wide_par, axis=1)
    gained_mine = (wide_mine * norm_gain.astype(F32)[None, :]).astype(BF)
    gained_par = (wide_par * gain_par.astype(F32)[None, :]).astype(BF)
    up = jnp.dot(gained_mine, up_weight, preferred_element_type=F32) + jnp.dot(
        gained_par, up_par, preferred_element_type=F32
    )
    sq_hi = squares.astype(BF)
    sq_lo = (squares - sq_hi.astype(F32)).astype(BF)
    tail = jnp.pad(jnp.stack([sq_hi, sq_lo], axis=1), ((0, 0), (0, 126)))
    sent = jnp.concatenate([up.astype(BF), tail], axis=1).reshape(8, 16, 4096 + 128)
    got = lax.all_to_all(sent, ("z", "xh"), 0, 0, tiled=True)
    total = jnp.sum(got.astype(F32), axis=0)
    row_sq = total[:, 4096] + total[:, 4097]
    verifier_up = total[:, :4096] * lax.rsqrt(row_sq / D + eps)[:, None]
    scores16 = jnp.sum(jax.nn.silu(verifier_up) * head_weight.astype(F32)[None, :], axis=1)

    pair = (local_prompt * CLUSTERS + cluster_ids).astype(F32)
    pair16 = lax.dynamic_slice_in_dim(pair, t * 16, 16, 0)
    mine = jnp.concatenate([scores16, pair16, jnp.zeros((96,), F32)])
    everyone = lax.all_to_all(jnp.broadcast_to(mine[None, :], (128, 128)), AXES, 0, 0, tiled=True)
    table = everyone.reshape(8, 2, 8, 128)
    all_scores = table[..., :16].transpose(2, 1, 0, 3).reshape(16, 128)
    all_pairs = table[..., 16:32].reshape(16, 128)
    hot = all_pairs[:, :, None] == jnp.arange(32, dtype=F32)[None, None, :]
    votes = jnp.sum(jnp.where(hot, all_scores[:, :, None], 0.0), axis=1)
    scores = lax.dynamic_slice_in_dim(all_scores.reshape(8, 256), t, 1, 0).reshape(256)
    return hidden, scores, votes.reshape(32, CLUSTERS)


def solution(mesh):
    fine = Mesh(mesh.devices.reshape(4, 2, 2, 2, 2, 2), AXES)
    placed = (
        P(DP, TP),
        P(DP, TP),
        P(DP, TP),
        P(DP, TP, None, None),
        P(DP, TP, None, None),
        P(DP),
        P(DP, TP, None, None),
        P(DP, TP, None, None),
        P(DP),
        P(DP),
        P(TP, DP),
        P(TP, DP),
        P(DP),
        P(DP, None),
        P(),
    )
    return jax.shard_map(
        body,
        mesh=fine,
        in_specs=placed,
        out_specs=(P(TP, DP), P(TP), P()),
        check_vma=False,
    )
```

```python
import functools
import math

import jax
import jax.numpy as jnp
from jax import lax
from jax.experimental import pallas as pl
from jax.experimental.pallas import tpu as pltpu
from jax.sharding import Mesh, PartitionSpec as P

D = 8192
CLUSTERS = 16
PROMPTS_DEV = 2
eps = 1e-05
AXES = ("z", "xh", "c", "xl", "yh", "yl")
DP = ("z", "xh", "c")
TP = ("xl", "yh", "yl")
BF = jnp.bfloat16
F32 = jnp.float32
SCALE2 = math.log2(math.e) / math.sqrt(128)
NEG = -1e30
NT = (((1,), (1,)), ((), ()))


def attn_kernel(rows, tile, ids_hbm, ids2_hbm, lens_hbm, q_hbm, nk_hbm, nv_hbm, pk_hbm, pv_hbm, ck_hbm, cv_hbm,
                out_ref, ids_s, ids_v, lens_v, q_ref, nk_ref, nv_ref, pk, pv, ck, cv, qs, nks, nvs, lens, acc,
                mbuf, lbuf, s_scr, sem_i, sem_p, sem_k, sem_v):
    small = [pltpu.make_async_copy(h, v, sem_i.at[i]) for i, (h, v) in enumerate((
        (ids_hbm, ids_s), (ids2_hbm, ids_v), (lens_hbm, lens_v), (q_hbm, q_ref), (nk_hbm, nk_ref), (nv_hbm, nv_ref)))]
    for cp in small:
        cp.start()
    heads = q_ref.shape[1] // 128
    tiles = rows // tile
    ctile = 16
    ctiles = rows // ctile
    keys = pk.shape[1]
    pre = [pltpu.make_async_copy(h.at[p], v.at[p], sem_p.at[p, i])
           for p in range(2) for i, (h, v) in enumerate(((pk_hbm, pk), (pv_hbm, pv)))]
    for cp in pre:
        cp.start()

    small[0].wait()

    def place(r, counts):
        c0, c1 = counts
        p = ids_s[r] & 1
        to = jnp.where(p == 0, c0, rows - 1 - c1)
        blk = to // ctile
        pltpu.make_async_copy(ck_hbm.at[r], ck.at[to], sem_k.at[blk]).start()
        pltpu.make_async_copy(cv_hbm.at[r], cv.at[to], sem_v.at[blk]).start()
        return c0 + 1 - p, c1 + p

    n0, _ = lax.fori_loop(0, rows, place, (jnp.int32(0), jnp.int32(0)), unroll=8)

    for cp in small[1:]:
        cp.wait()
    second = (ids_v[...] & 1)
    ones = jnp.broadcast_to(second, (rows, rows)).astype(F32).astype(BF)
    ri = lax.broadcasted_iota(jnp.int32, (rows, rows), 0)
    ci = lax.broadcasted_iota(jnp.int32, (rows, rows), 1)
    upper = (ri < ci).astype(F32).astype(BF)
    before1 = jnp.dot(ones, upper, preferred_element_type=F32)
    pos = jnp.where(jnp.broadcast_to(second, (rows, rows)) == 0, ci.astype(F32) - before1, rows - 1 - before1)
    perm32 = (pos == ri.astype(F32)).astype(F32)
    perm = perm32.astype(BF)
    unperm = perm32.T.astype(BF)
    qs[...] = jnp.dot(perm, q_ref[...], preferred_element_type=F32).astype(BF)
    nks[...] = jnp.dot(perm, nk_ref[...], preferred_element_type=F32)
    nvs[...] = jnp.dot(perm, nv_ref[...], preferred_element_type=F32)
    lb = jnp.broadcast_to(lens_v[...], (128, rows)).astype(F32).astype(BF)
    lens[...] = lax.dot_general(perm, lb, NT, preferred_element_type=F32)

    for cp in pre:
        cp.wait()
    edge = jnp.minimum(n0 // tile, tiles - 1)
    chunk = 512

    def prefix(item, _):
        p = (item > edge).astype(jnp.int32)
        row0 = pl.multiple_of((item - p) * tile, tile)
        qt = jnp.concatenate([qs[pl.ds(row0, tile), h * 128:(h + 1) * 128] for h in range(heads)], axis=0)
        top = None
        for k in range(0, keys, chunk):
            s = lax.dot_general(qt, pk[p, k:k + chunk], NT, preferred_element_type=F32)
            s_scr[:, k:k + chunk] = s
            for j in range(0, chunk, 128):
                top = s[:, j:j + 128] if top is None else jnp.maximum(top, s[:, j:j + 128])
        m = jnp.max(top, axis=1, keepdims=True)
        mb = jnp.broadcast_to(m, (heads * tile, 128))
        l = jnp.zeros((heads * tile, 128), F32)
        o = jnp.zeros((heads * tile, 128), F32)
        for k in range(0, keys, chunk):
            ps = []
            for j in range(0, chunk, 128):
                e = jnp.exp2((s_scr[:, k + j:k + j + 128] - mb) * SCALE2)
                l = l + e
                ps.append(e.astype(BF))
            o = o + jnp.dot(jnp.concatenate(ps, axis=1), pv[p, k:k + chunk], preferred_element_type=F32)
        lsum = jnp.broadcast_to(jnp.sum(l, axis=1, keepdims=True), (heads * tile, 128))
        at = row0 + lax.broadcasted_iota(jnp.int32, (tile, 128), 0)
        mine = (at < n0) == (p == 0)
        for h in range(heads):
            hs = slice(h * tile, (h + 1) * tile)
            cs = slice(h * 128, (h + 1) * 128)
            rs = pl.ds(row0, tile)
            acc[rs, cs] = jnp.where(mine, o[hs], acc[rs, cs])
            mbuf[rs, cs] = jnp.where(mine, mb[hs], mbuf[rs, cs])
            lbuf[rs, cs] = jnp.where(mine, lsum[hs], lbuf[rs, cs])
        return 0

    lax.fori_loop(0, tiles + 1, prefix, 0)

    mrow = lax.broadcasted_iota(jnp.int32, (heads * ctile, 128), 0) % ctile
    lane = lax.broadcasted_iota(jnp.int32, (heads * ctile, 128), 1).astype(F32)

    def cached(b, _):
        r0 = pl.multiple_of(b * ctile, ctile)
        rs = pl.ds(r0, ctile)
        pltpu.make_async_copy(ck_hbm.at[pl.ds(0, ctile)], ck.at[rs], sem_k.at[b]).wait()
        pltpu.make_async_copy(cv_hbm.at[pl.ds(0, ctile)], cv.at[rs], sem_v.at[b]).wait()
        heads_of = lambda ref: jnp.concatenate([ref[rs, h * 128:(h + 1) * 128] for h in range(heads)], axis=0)
        rep = lambda x: jnp.concatenate([x] * heads, axis=0)
        qt = heads_of(qs)
        kt = ck[rs].reshape(ctile * 128, 128)
        vt = cv[rs].reshape(ctile * 128, 128)
        s = lax.dot_general(qt, kt, NT, preferred_element_type=F32)
        sc = s[:, :128]
        for r in range(1, ctile):
            sc = jnp.where(mrow == r, s[:, r * 128:(r + 1) * 128], sc)
        sc = jnp.where(lane < rep(lens[rs]), sc, NEG)
        so = jnp.sum(qt.astype(F32) * rep(nks[rs]), axis=1, keepdims=True)
        mp = heads_of(mbuf)
        m = jnp.maximum(jnp.maximum(mp, jnp.max(sc, axis=1, keepdims=True)), so)
        ap = jnp.exp2((mp - m) * SCALE2)
        e = jnp.exp2((sc - m) * SCALE2)
        eo = jnp.exp2((so - m) * SCALE2)
        eb = e.astype(BF).astype(F32)
        pe = jnp.concatenate([jnp.where(mrow == r, eb, 0.0).astype(BF) for r in range(ctile)], axis=1)
        oc = jnp.dot(pe, vt, preferred_element_type=F32)
        l = ap * heads_of(lbuf) + jnp.sum(e, axis=1, keepdims=True) + eo
        o = (ap * heads_of(acc) + oc + eo * rep(nvs[rs])) / l
        for h in range(heads):
            qs[rs, h * 128:(h + 1) * 128] = o[h * ctile:(h + 1) * ctile].astype(BF)
        return 0

    lax.fori_loop(0, ctiles, cached, 0)
    out_ref[...] = jnp.dot(unperm, qs[...], preferred_element_type=F32).astype(BF)


def attend(queries, new_key, new_value, ck, cv, lengths, pk, pv, prompt_ids, tile=32):
    rows = queries.shape[0]
    width = queries.shape[1]
    keys = pk.shape[2]
    heads = width // 128
    V = pl.BlockSpec(memory_space=pltpu.VMEM)
    A = pl.BlockSpec(memory_space=pl.ANY)
    S = pl.BlockSpec(memory_space=pltpu.SMEM)
    return pl.pallas_call(
        functools.partial(attn_kernel, rows, tile),
        out_shape=jax.ShapeDtypeStruct((rows, width), BF),
        in_specs=[A] * 10,
        out_specs=V,
        scratch_shapes=[
            pltpu.SMEM((rows,), jnp.int32), pltpu.VMEM((1, rows), jnp.int32), pltpu.VMEM((1, rows), jnp.int32),
            pltpu.VMEM((rows, width), BF), pltpu.VMEM((rows, 128), BF), pltpu.VMEM((rows, 128), BF),
            pltpu.VMEM((2, keys, 128), BF), pltpu.VMEM((2, keys, 128), BF),
            pltpu.VMEM((rows, 128, 128), BF), pltpu.VMEM((rows, 128, 128), BF),
            pltpu.VMEM((rows, width), BF), pltpu.VMEM((rows, 128), F32), pltpu.VMEM((rows, 128), F32),
            pltpu.VMEM((rows, 128), F32),
            pltpu.VMEM((rows, width), F32), pltpu.VMEM((rows, width), F32), pltpu.VMEM((rows, width), F32),
            pltpu.VMEM((heads * tile, keys), F32),
            pltpu.SemaphoreType.DMA((6,)), pltpu.SemaphoreType.DMA((2, 2)), pltpu.SemaphoreType.DMA((rows // 16,)), pltpu.SemaphoreType.DMA((rows // 16,)),
        ],
        compiler_params=pltpu.CompilerParams(vmem_limit_bytes=58 * 1024 * 1024),
        cost_estimate=pl.CostEstimate(flops=2*2*1024*2048*128*2, bytes_accessed=11*1024*1024, transcendentals=2*1024*1024),
    )(prompt_ids, prompt_ids.reshape(1, rows), lengths.reshape(1, rows), queries, new_key, new_value,
      pk.reshape(2, keys, 128), pv.reshape(2, keys, 128), ck.reshape(rows, 128, 128), cv.reshape(rows, 128, 128))


def swap(x, axis):
    return lax.ppermute(x, axis, [(0, 1), (1, 0)])


def shift(x, by):
    return lax.ppermute(x, "z", [(i, (i + by) % 4) for i in range(4)])


def proj_kernel(z_ref, here, before, after, far_a, far_b, w00, w01, w10, w11, out_ref):
    step = pl.program_id(0)

    def work(a, rows):
        own, par = a[:, :1024], a[:, 1024:]
        for j, (wo, wp) in enumerate(((w00, w10), (w01, w11))):
            acc = jnp.dot(own, wo[...], preferred_element_type=F32)
            acc = acc + jnp.dot(par, wp[...], preferred_element_type=F32)
            out_ref[0, rows, j * 512 : (j + 1) * 512] = acc.astype(BF)

    full = slice(0, 128)

    @pl.when(step == 0)
    def _():
        work(here[...], full)

    @pl.when(step == 1)
    def _():
        work(before[...], full)

    @pl.when(step == 2)
    def _():
        work(jnp.concatenate([far_a[...], far_b[...]], axis=0), full)

    @pl.when(step == 3)
    def _():
        work(after[...], full)


def project(here, before, after, far_a, far_b, w00, w01, w10, w11):
    z = lax.axis_index("z").astype(jnp.int32).reshape(1)
    whole = lambda a: pl.BlockSpec(a.shape, lambda s, z_ref: (0,) * a.ndim)
    ins = (here, before, after, far_a, far_b, w00, w01, w10, w11)
    return pl.pallas_call(
        proj_kernel,
        out_shape=jax.ShapeDtypeStruct((4, 128, 1024), BF),
        grid_spec=pltpu.PrefetchScalarGridSpec(
            num_scalar_prefetch=1,
            grid=(4,),
            in_specs=[whole(a) for a in ins],
            out_specs=pl.BlockSpec((1, 128, 1024), lambda s, z_ref: ((z_ref[0] + 4 - s) % 4, 0, 0)),
        ),
        compiler_params=pltpu.CompilerParams(vmem_limit_bytes=40 * 1024 * 1024),
        cost_estimate=pl.CostEstimate(
            flops=2 * 512 * 2048 * 1024, bytes_accessed=7 * 1024 * 1024, transcendentals=0
        ),
    )(z, *ins)


def body(
    queries,
    new_key,
    new_value,
    cache_keys,
    cache_values,
    lengths,
    prefix_keys,
    prefix_values,
    prompt_ids,
    cluster_ids,
    out_weight,
    residual,
    norm_gain,
    up_weight,
    head_weight,
):
    c = lax.axis_index("c")
    xh = lax.axis_index("xh")
    yl = lax.axis_index("yl")
    t = lax.axis_index(TP)
    dp_index = lax.axis_index(DP)
    local_prompt = prompt_ids - dp_index * PROMPTS_DEV

    w00 = out_weight
    w10 = swap(out_weight, "yl")
    w01 = swap(w00, "c")
    w11 = swap(w10, "c")
    up_par = swap(up_weight, "c")
    res_mine = lax.dynamic_slice_in_dim(residual, c * 128, 128, 0)
    res_send = lax.dynamic_slice_in_dim(residual, (1 - c) * 128, 128, 0)
    extra = swap(
        jnp.concatenate([res_send, jnp.broadcast_to(norm_gain[None, :], (16, 512))], axis=0), "c"
    )
    res_par, gain_par = extra[:128], extra[128]

    attended = attend(
        queries,
        new_key,
        new_value,
        cache_keys,
        cache_values,
        lengths,
        prefix_keys,
        prefix_values,
        prompt_ids,
    )

    first = lax.ppermute(attended, ("xh", "yl"), [(0, 2), (3, 1), (1, 0), (2, 3)])
    second = lax.ppermute(attended, ("xh", "yl"), [(1, 2), (2, 1)])
    diagonal = xh == yl
    here = jnp.concatenate(
        [jnp.where(diagonal, attended, first), jnp.where(diagonal, first, second)], axis=1
    )
    before = shift(here, 1)
    after = shift(here, -1)
    far_a = shift(before[:64], 1)
    far_b = shift(after[64:], -1)
    partial = project(here, before, after, far_a, far_b, w00, w01, w10, w11)
    parts = lax.all_to_all(partial, ("xl", "yh"), 0, 0, tiled=True)
    mixed = jnp.sum(parts.astype(F32), axis=0)
    hid_mine = (res_mine.astype(F32) + mixed[:, :512]).astype(BF)
    hid_par = (res_par.astype(F32) + mixed[:, 512:]).astype(BF)
    hid_back = swap(hid_par, "c")
    hidden = jnp.where(
        c == 0,
        jnp.concatenate([hid_mine, hid_back], axis=0),
        jnp.concatenate([hid_back, hid_mine], axis=0),
    )

    wide_mine, wide_par = hid_mine.astype(F32), hid_par.astype(F32)
    squares = jnp.sum(wide_mine * wide_mine, axis=1) + jnp.sum(wide_par * wide_par, axis=1)
    gained_mine = (wide_mine * norm_gain.astype(F32)[None, :]).astype(BF)
    gained_par = (wide_par * gain_par.astype(F32)[None, :]).astype(BF)
    up = jnp.dot(gained_mine, up_weight, preferred_element_type=F32) + jnp.dot(
        gained_par, up_par, preferred_element_type=F32
    )
    sq_hi = squares.astype(BF)
    sq_lo = (squares - sq_hi.astype(F32)).astype(BF)
    tail = jnp.pad(jnp.stack([sq_hi, sq_lo], axis=1), ((0, 0), (0, 126)))
    sent = jnp.concatenate([up.astype(BF), tail], axis=1).reshape(8, 16, 4096 + 128)
    got = lax.all_to_all(sent, ("z", "xh"), 0, 0, tiled=True)
    total = jnp.sum(got.astype(F32), axis=0)
    row_sq = total[:, 4096] + total[:, 4097]
    verifier_up = total[:, :4096] * lax.rsqrt(row_sq / D + eps)[:, None]
    scores16 = jnp.sum(jax.nn.silu(verifier_up) * head_weight.astype(F32)[None, :], axis=1)

    pair = (local_prompt * CLUSTERS + cluster_ids).astype(F32)
    pair16 = lax.dynamic_slice_in_dim(pair, t * 16, 16, 0)
    mine = jnp.concatenate([scores16, pair16, jnp.zeros((96,), F32)])
    everyone = lax.all_to_all(jnp.broadcast_to(mine[None, :], (128, 128)), AXES, 0, 0, tiled=True)
    table = everyone.reshape(8, 2, 8, 128)
    all_scores = table[..., :16].transpose(2, 1, 0, 3).reshape(16, 128)
    all_pairs = table[..., 16:32].reshape(16, 128)
    hot = all_pairs[:, :, None] == jnp.arange(32, dtype=F32)[None, None, :]
    votes = jnp.sum(jnp.where(hot, all_scores[:, :, None], 0.0), axis=1)
    scores = lax.dynamic_slice_in_dim(all_scores.reshape(8, 256), t, 1, 0).reshape(256)
    return hidden, scores, votes.reshape(32, CLUSTERS)


def solution(mesh):
    fine = Mesh(mesh.devices.reshape(4, 2, 2, 2, 2, 2), AXES)
    placed = (
        P(DP, TP),
        P(DP, TP),
        P(DP, TP),
        P(DP, TP, None, None),
        P(DP, TP, None, None),
        P(DP),
        P(DP, TP, None, None),
        P(DP, TP, None, None),
        P(DP),
        P(DP),
        P(TP, DP),
        P(TP, DP),
        P(DP),
        P(DP, None),
        P(),
    )
    return jax.shard_map(
        body,
        mesh=fine,
        in_specs=placed,
        out_specs=(P(TP, DP), P(TP), P()),
        check_vma=False,
    )
```

```python
import functools
import math

import jax
import jax.numpy as jnp
from jax import lax
from jax.experimental import pallas as pl
from jax.experimental.pallas import tpu as pltpu
from jax.sharding import Mesh, PartitionSpec as P

D = 8192
CLUSTERS = 16
PROMPTS_DEV = 2
eps = 1e-05
AXES = ("z", "xh", "c", "xl", "yh", "yl")
DP = ("z", "xh", "c")
TP = ("xl", "yh", "yl")
BF = jnp.bfloat16
F32 = jnp.float32
SCALE2 = math.log2(math.e) / math.sqrt(128)
NEG = -1e30
LIMIT = 63 * 1024 * 1024
NT = (((1,), (1,)), ((), ()))


def attn_kernel(rows, tile, ids_hbm, ids2_hbm, lens_hbm, q_hbm, nk_hbm, nv_hbm, pk_hbm, pv_hbm, ck_hbm, cv_hbm,
                out_ref, ids_s, ids_v, lens_v, q_ref, nk_ref, nv_ref, pk, pv, ck, cv, qs, nks, nvs, lens, acc,
                mbuf, lbuf, s_scr, sem_i, sem_p, sem_k, sem_v):
    small = [pltpu.make_async_copy(h, v, sem_i.at[i]) for i, (h, v) in enumerate((
        (ids_hbm, ids_s), (ids2_hbm, ids_v), (lens_hbm, lens_v), (q_hbm, q_ref), (nk_hbm, nk_ref), (nv_hbm, nv_ref)))]
    for cp in small:
        cp.start()
    heads = q_ref.shape[1] // 128
    tiles = rows // tile
    ctile = 16
    ctiles = rows // ctile
    keys = pk.shape[1]
    pre = [pltpu.make_async_copy(h.at[p], v.at[p], sem_p.at[p, i])
           for p in range(2) for i, (h, v) in enumerate(((pk_hbm, pk), (pv_hbm, pv)))]
    for cp in pre:
        cp.start()

    small[0].wait()

    def place(r, counts):
        c0, c1 = counts
        p = ids_s[r] & 1
        to = jnp.where(p == 0, c0, rows - 1 - c1)
        blk = to // ctile
        pltpu.make_async_copy(ck_hbm.at[r], ck.at[to], sem_k.at[blk]).start()
        pltpu.make_async_copy(cv_hbm.at[r], cv.at[to], sem_v.at[blk]).start()
        return c0 + 1 - p, c1 + p

    n0, _ = lax.fori_loop(0, rows, place, (jnp.int32(0), jnp.int32(0)), unroll=8)

    for cp in small[1:]:
        cp.wait()
    second = (ids_v[...] & 1)
    ones = jnp.broadcast_to(second, (rows, rows)).astype(F32).astype(BF)
    ri = lax.broadcasted_iota(jnp.int32, (rows, rows), 0)
    ci = lax.broadcasted_iota(jnp.int32, (rows, rows), 1)
    upper = (ri < ci).astype(F32).astype(BF)
    before1 = jnp.dot(ones, upper, preferred_element_type=F32)
    pos = jnp.where(jnp.broadcast_to(second, (rows, rows)) == 0, ci.astype(F32) - before1, rows - 1 - before1)
    perm32 = (pos == ri.astype(F32)).astype(F32)
    perm = perm32.astype(BF)
    unperm = perm32.T.astype(BF)
    qs[...] = jnp.dot(perm, q_ref[...], preferred_element_type=F32).astype(BF)
    nks[...] = jnp.dot(perm, nk_ref[...], preferred_element_type=F32)
    nvs[...] = jnp.dot(perm, nv_ref[...], preferred_element_type=F32)
    lb = jnp.broadcast_to(lens_v[...], (128, rows)).astype(F32).astype(BF)
    lens[...] = lax.dot_general(perm, lb, NT, preferred_element_type=F32)

    for cp in pre:
        cp.wait()
    edge = jnp.minimum(n0 // tile, tiles - 1)
    chunk = 512

    def prefix(item, _):
        p = (item > edge).astype(jnp.int32)
        row0 = pl.multiple_of((item - p) * tile, tile)
        qt = jnp.concatenate([qs[pl.ds(row0, tile), h * 128:(h + 1) * 128] for h in range(heads)], axis=0)
        top = None
        for k in range(0, keys, chunk):
            s = lax.dot_general(qt, pk[p, k:k + chunk], NT, preferred_element_type=F32)
            s_scr[:, k:k + chunk] = s
            for j in range(0, chunk, 128):
                top = s[:, j:j + 128] if top is None else jnp.maximum(top, s[:, j:j + 128])
        m = jnp.max(top, axis=1, keepdims=True)
        mb = jnp.broadcast_to(m, (heads * tile, 128))
        l = jnp.zeros((heads * tile, 128), F32)
        o = jnp.zeros((heads * tile, 128), F32)
        for k in range(0, keys, chunk):
            ps = []
            for j in range(0, chunk, 128):
                e = jnp.exp2((s_scr[:, k + j:k + j + 128] - mb) * SCALE2)
                l = l + e
                ps.append(e.astype(BF))
            o = o + jnp.dot(jnp.concatenate(ps, axis=1), pv[p, k:k + chunk], preferred_element_type=F32)
        lsum = jnp.broadcast_to(jnp.sum(l, axis=1, keepdims=True), (heads * tile, 128))
        at = row0 + lax.broadcasted_iota(jnp.int32, (tile, 128), 0)
        mine = (at < n0) == (p == 0)
        for h in range(heads):
            hs = slice(h * tile, (h + 1) * tile)
            cs = slice(h * 128, (h + 1) * 128)
            rs = pl.ds(row0, tile)
            acc[rs, cs] = jnp.where(mine, o[hs], acc[rs, cs])
            mbuf[rs, cs] = jnp.where(mine, mb[hs], mbuf[rs, cs])
            lbuf[rs, cs] = jnp.where(mine, lsum[hs], lbuf[rs, cs])
        return 0

    lax.fori_loop(0, tiles + 1, prefix, 0)

    mrow = lax.broadcasted_iota(jnp.int32, (heads * ctile, 128), 0) % ctile
    lane = lax.broadcasted_iota(jnp.int32, (heads * ctile, 128), 1).astype(F32)

    def cached(b, _):
        r0 = pl.multiple_of(b * ctile, ctile)
        rs = pl.ds(r0, ctile)
        pltpu.make_async_copy(ck_hbm.at[pl.ds(0, ctile)], ck.at[rs], sem_k.at[b]).wait()
        pltpu.make_async_copy(cv_hbm.at[pl.ds(0, ctile)], cv.at[rs], sem_v.at[b]).wait()
        heads_of = lambda ref: jnp.concatenate([ref[rs, h * 128:(h + 1) * 128] for h in range(heads)], axis=0)
        rep = lambda x: jnp.concatenate([x] * heads, axis=0)
        qt = heads_of(qs)
        kt = ck[rs].reshape(ctile * 128, 128)
        vt = cv[rs].reshape(ctile * 128, 128)
        s = lax.dot_general(qt, kt, NT, preferred_element_type=F32)
        sc = s[:, :128]
        for r in range(1, ctile):
            sc = jnp.where(mrow == r, s[:, r * 128:(r + 1) * 128], sc)
        sc = jnp.where(lane < rep(lens[rs]), sc, NEG)
        so = jnp.sum(qt.astype(F32) * rep(nks[rs]), axis=1, keepdims=True)
        mp = heads_of(mbuf)
        m = jnp.maximum(jnp.maximum(mp, jnp.max(sc, axis=1, keepdims=True)), so)
        ap = jnp.exp2((mp - m) * SCALE2)
        e = jnp.exp2((sc - m) * SCALE2)
        eo = jnp.exp2((so - m) * SCALE2)
        eb = e.astype(BF).astype(F32)
        pe = jnp.concatenate([jnp.where(mrow == r, eb, 0.0).astype(BF) for r in range(ctile)], axis=1)
        oc = jnp.dot(pe, vt, preferred_element_type=F32)
        l = ap * heads_of(lbuf) + jnp.sum(e, axis=1, keepdims=True) + eo
        o = (ap * heads_of(acc) + oc + eo * rep(nvs[rs])) / l
        for h in range(heads):
            qs[rs, h * 128:(h + 1) * 128] = o[h * ctile:(h + 1) * ctile].astype(BF)
        return 0

    lax.fori_loop(0, ctiles, cached, 0)
    out_ref[...] = jnp.dot(unperm, qs[...], preferred_element_type=F32).astype(BF)


def attend(queries, new_key, new_value, ck, cv, lengths, pk, pv, prompt_ids, tile=32):
    rows = queries.shape[0]
    width = queries.shape[1]
    keys = pk.shape[2]
    heads = width // 128
    V = pl.BlockSpec(memory_space=pltpu.VMEM)
    A = pl.BlockSpec(memory_space=pl.ANY)
    S = pl.BlockSpec(memory_space=pltpu.SMEM)
    return pl.pallas_call(
        functools.partial(attn_kernel, rows, tile),
        out_shape=jax.ShapeDtypeStruct((rows, width), BF),
        in_specs=[A] * 10,
        out_specs=V,
        scratch_shapes=[
            pltpu.SMEM((rows,), jnp.int32), pltpu.VMEM((1, rows), jnp.int32), pltpu.VMEM((1, rows), jnp.int32),
            pltpu.VMEM((rows, width), BF), pltpu.VMEM((rows, 128), BF), pltpu.VMEM((rows, 128), BF),
            pltpu.VMEM((2, keys, 128), BF), pltpu.VMEM((2, keys, 128), BF),
            pltpu.VMEM((rows, 128, 128), BF), pltpu.VMEM((rows, 128, 128), BF),
            pltpu.VMEM((rows, width), BF), pltpu.VMEM((rows, 128), F32), pltpu.VMEM((rows, 128), F32),
            pltpu.VMEM((rows, 128), F32),
            pltpu.VMEM((rows, width), F32), pltpu.VMEM((rows, width), F32), pltpu.VMEM((rows, width), F32),
            pltpu.VMEM((heads * tile, keys), F32),
            pltpu.SemaphoreType.DMA((6,)), pltpu.SemaphoreType.DMA((2, 2)), pltpu.SemaphoreType.DMA((rows // 16,)), pltpu.SemaphoreType.DMA((rows // 16,)),
        ],
        compiler_params=pltpu.CompilerParams(vmem_limit_bytes=LIMIT),
        cost_estimate=pl.CostEstimate(flops=16 * 10**9, bytes_accessed=11 * 1024 * 1024, transcendentals=2 * 1024 * 1024),
    )(prompt_ids, prompt_ids.reshape(1, rows), lengths.reshape(1, rows), queries, new_key, new_value,
      pk.reshape(2, keys, 128), pv.reshape(2, keys, 128), ck.reshape(rows, 128, 128), cv.reshape(rows, 128, 128))


def swap(x, axis):
    return lax.ppermute(x, axis, [(0, 1), (1, 0)])


def shift(x, by):
    return lax.ppermute(x, "z", [(i, (i + by) % 4) for i in range(4)])


def tiny(mib, flops=1024, **kw):
    return dict(
        compiler_params=pltpu.CompilerParams(vmem_limit_bytes=mib * 1024 * 1024),
        cost_estimate=pl.CostEstimate(flops=flops, bytes_accessed=1024, transcendentals=0),
        **kw,
    )


def hold_kernel(*refs):
    pass


def hold(x, *tokens):
    A = pl.BlockSpec(memory_space=pl.ANY)
    return pl.pallas_call(
        hold_kernel,
        out_shape=jax.ShapeDtypeStruct(x.shape, x.dtype),
        in_specs=[A] * (1 + len(tokens)),
        out_specs=A,
        input_output_aliases={0: 0},
        **tiny(4),
    )(x, *tokens)


def proj_kernel(steps, *refs):
    count = len(steps)
    rows, weights = refs[:count], refs[count : count + 4]
    out, w, chunks, sems = refs[-4:]
    loads = [
        pltpu.make_async_copy(src, w.at[:, j * 512 : (j + 1) * 512], sems.at[j])
        for j, src in enumerate(weights)
    ]
    for load in loads:
        load.start()
    a = jnp.concatenate([row[...] for row in rows], axis=0)
    z = lax.axis_index("z")
    xh = lax.axis_index("xh")
    leave = []
    for j in range(4):
        loads[j].wait()
        total = jnp.dot(a, w[:, j * 512 : (j + 1) * 512], preferred_element_type=F32).astype(BF)
        total = total.reshape(count, 2, 64, 512)
        for i in range(count):
            chunks[j // 2, i, :, :, (j % 2) * 512 : (j % 2 + 1) * 512] = total[i]
        if j % 2:
            for i, step in enumerate(steps):
                first = ((xh ^ (j // 2)) * 4 + ((z - step) & 3)) * 2
                leave.append(
                    pltpu.make_async_copy(chunks.at[j // 2, i], out.at[pl.ds(first, 2)], sems.at[4 + j // 2 * count + i])
                )
                leave[-1].start()
    for copy in leave:
        copy.wait()


def project(steps, *ins):
    count = len(steps)
    more = len(ins) > count + 4
    V = pl.BlockSpec(memory_space=pltpu.VMEM)
    A = pl.BlockSpec(memory_space=pl.ANY)
    return pl.pallas_call(
        functools.partial(proj_kernel, steps),
        out_shape=jax.ShapeDtypeStruct((16, 64, 1024), BF),
        in_specs=[V] * count + [A] * (len(ins) - count),
        out_specs=A,
        input_output_aliases={count + 4: 0} if more else {},
        scratch_shapes=[
            pltpu.VMEM((1024, 2048), BF),
            pltpu.VMEM((2, count, 2, 64, 1024), BF),
            pltpu.SemaphoreType.DMA((4 + 2 * count,)),
        ],
        **tiny(40, 0 if more else 4 * 10**9),
    )(*ins)


def up_kernel(
    parts, res, extra, res_y, gain, up_mine, up_par,
    hm_ref, hp_ref, sent_ref, parts_v, res_v, gain_v, gain2_v, w, sems,
):
    c = lax.axis_index("c")
    yl = lax.axis_index("yl")
    here = pl.ds(pl.multiple_of(yl * 64, 64), 64)
    there = pl.ds(pl.multiple_of(64 - yl * 64, 64), 64)
    small = [
        pltpu.make_async_copy(src, dst, sems.at[i // 4, i % 4])
        for i, (src, dst) in enumerate((
            (parts.at[:8], parts_v.at[:8]), (parts.at[8:], parts_v.at[8:]),
            (res.at[pl.ds(pl.multiple_of(c * 128 + yl * 64, 64), 64)], res_v.at[here, :512]),
            (extra.at[here], res_v.at[here, 512:]),
            (res_y, res_v.at[there]),
            (gain, gain_v), (extra.at[128:], gain2_v),
        ))
    ]
    for copy in small:
        copy.start()
    loads = []
    for j in range(4):
        cols = slice(j * 1024, (j + 1) * 1024)
        loads.append((
            pltpu.make_async_copy(up_mine.at[:, cols], w.at[0:512, cols], sems.at[2, j]),
            pltpu.make_async_copy(up_par.at[:, cols], w.at[512:1024, cols], sems.at[3, j]),
        ))
        for load in loads[-1]:
            load.start()
    for copy in small:
        copy.wait()

    def summed(first):
        total = parts_v[first].astype(F32)
        for i in range(1, 8):
            total = total + parts_v[first + i].astype(F32)
        return total

    mixed = jnp.concatenate([summed(0), summed(8)], axis=0)
    hid = (res_v[...].astype(F32) + mixed).astype(BF)
    hm_ref[...] = hid[:, :512]
    hp_ref[...] = hid[:, 512:]
    wide = hid.astype(F32)
    squares = jnp.sum(wide * wide, axis=1, keepdims=True)
    hi = squares.astype(BF).astype(F32)
    lane = lax.broadcasted_iota(jnp.int32, (128, 128), 1)
    sent_ref[:, 4096:] = jnp.where(lane == 0, hi, jnp.where(lane == 1, squares - hi, 0.0)).astype(BF)
    gains = jnp.concatenate([gain_v[0:1], gain2_v[0:1]], axis=1).astype(F32)
    gained = (wide * gains).astype(BF)
    for j in range(4):
        cols = slice(j * 1024, (j + 1) * 1024)
        for load in loads[j]:
            load.wait()
        sent_ref[:, cols] = jnp.dot(gained, w[:, cols], preferred_element_type=F32).astype(BF)


def verify_up(*ins):
    V = pl.BlockSpec(memory_space=pltpu.VMEM)
    A = pl.BlockSpec(memory_space=pl.ANY)
    return pl.pallas_call(
        up_kernel,
        out_shape=(
            jax.ShapeDtypeStruct((128, 512), BF),
            jax.ShapeDtypeStruct((128, 512), BF),
            jax.ShapeDtypeStruct((128, 4096 + 128), BF),
        ),
        in_specs=[A] * 7,
        out_specs=(V, V, V),
        scratch_shapes=[
            pltpu.VMEM((16, 64, 1024), BF),
            pltpu.VMEM((128, 1024), BF),
            pltpu.VMEM((16, 512), BF),
            pltpu.VMEM((16, 512), BF),
            pltpu.VMEM((1024, 4096), BF),
            pltpu.SemaphoreType.DMA((4, 4)),
        ],
        **tiny(58),
    )(*ins)


def score_kernel(got_hbm, head_hbm, prompts_hbm, clusters_hbm, out_ref, got, head, prompts, clusters, sems):
    copies = [
        pltpu.make_async_copy(src, dst, sems.at[i])
        for i, (src, dst) in enumerate((
            (got_hbm, got), (head_hbm, head), (prompts_hbm, prompts), (clusters_hbm, clusters)
        ))
    ]
    for copy in copies:
        copy.start()
    for copy in copies:
        copy.wait()

    def summed(cols):
        total = got[0, :, cols].astype(F32)
        for i in range(1, 8):
            total = total + got[i, :, cols].astype(F32)
        return total

    tail = summed(slice(4096, 4224))
    squares = tail[:, 0:1] + tail[:, 1:2]
    factor = lax.rsqrt(squares / D + eps)
    acc = jnp.zeros((16, 512), F32)
    for j in range(0, 4096, 512):
        cols = slice(j, j + 512)
        up = summed(cols) * factor
        acc = acc + up / (1.0 + jnp.exp(-up)) * head[0:1, cols].astype(F32)
    scores = jnp.sum(acc, axis=1, keepdims=True)
    row = lax.broadcasted_iota(jnp.int32, (16, 128), 0)
    lane = lax.broadcasted_iota(jnp.int32, (16, 128), 1)
    line = jnp.sum(jnp.where(row == lane, scores, 0.0), axis=0, keepdims=True)
    pair = ((prompts[...] & 1) * CLUSTERS + clusters[...]).astype(F32)
    t = lax.axis_index(TP)
    pair = pltpu.roll(jnp.broadcast_to(pair, (8, 128)), (144 - t * 16) & 127, 1)[0:1]
    lane = lane[0:1]
    mine = jnp.where(lane < 16, line, jnp.where(lane < 32, pair, 0.0))
    out_ref[...] = jnp.broadcast_to(mine.reshape(1, 1, 128), (128, 1, 128))


def score(got, head_weight, prompt_ids, cluster_ids):
    V = pl.BlockSpec(memory_space=pltpu.VMEM)
    A = pl.BlockSpec(memory_space=pl.ANY)
    return pl.pallas_call(
        score_kernel,
        out_shape=jax.ShapeDtypeStruct((128, 1, 128), F32),
        in_specs=[A] * 4,
        out_specs=V,
        scratch_shapes=[
            pltpu.VMEM((8, 16, 4096 + 128), BF),
            pltpu.VMEM((1, 4096), BF),
            pltpu.VMEM((1, 128), jnp.int32),
            pltpu.VMEM((1, 128), jnp.int32),
            pltpu.SemaphoreType.DMA((4,)),
        ],
        **tiny(40),
    )(got, head_weight.reshape(1, 4096), prompt_ids.reshape(1, 128), cluster_ids.reshape(1, 128))


def vote_kernel(all_hbm, scores_ref, votes_ref, x3, x, sem):
    copy = pltpu.make_async_copy(all_hbm, x3, sem)
    copy.start()
    copy.wait()
    x[...] = x3[...].reshape(128, 128)
    t = lax.axis_index(TP)
    lane8 = lax.broadcasted_iota(jnp.int32, (8, 128), 1)
    lane = lax.broadcasted_iota(jnp.int32, (16, 32), 1)
    row = lax.broadcasted_iota(jnp.int32, (16, 32), 0)

    def scores_of(zx, c):
        base = (zx & 1) * 64 + c * 8 + (zx >> 1) * 2
        return jnp.concatenate(
            [x[pl.ds(base, 4, stride=16), :], x[pl.ds(base + 1, 4, stride=16), :]], axis=0
        )

    for c in range(2):
        block = jnp.where(lane8 < 16, scores_of(t, c), 0.0)
        spread = block[0:1]
        for i in range(1, 8):
            spread = spread + pltpu.roll(block, 16 * i, 1)[i : i + 1]
        scores_ref[c : c + 1, :] = spread
    live = (lane8 >= 16) & (lane8 < 32)
    votes = jnp.zeros((16, 32), F32)
    for zx in range(8):
        for c in range(2):
            dp = zx * 2 + c
            ids = jnp.where(live, x[dp * 8 : dp * 8 + 8, :], -1.0)
            vals = pltpu.roll(scores_of(zx, c), 16, 1)
            for p in range(2):
                for k in range(CLUSTERS):
                    hit = jnp.where(ids == float(p * CLUSTERS + k), vals, 0.0)
                    one = jnp.sum(jnp.sum(hit, axis=0, keepdims=True), axis=1, keepdims=True)
                    votes = jnp.where((row == k) & (lane == dp * 2 + p), one, votes)
    votes_ref[...] = votes


def tally(everyone):
    V = pl.BlockSpec(memory_space=pltpu.VMEM)
    A = pl.BlockSpec(memory_space=pl.ANY)
    return pl.pallas_call(
        vote_kernel,
        out_shape=(jax.ShapeDtypeStruct((2, 128), F32), jax.ShapeDtypeStruct((CLUSTERS, 32), F32)),
        in_specs=[A],
        out_specs=(V, V),
        scratch_shapes=[pltpu.VMEM((128, 1, 128), F32), pltpu.VMEM((128, 128), F32), pltpu.SemaphoreType.DMA],
        **tiny(40),
    )(everyone)


def body(
    queries,
    new_key,
    new_value,
    cache_keys,
    cache_values,
    lengths,
    prefix_keys,
    prefix_values,
    prompt_ids,
    cluster_ids,
    out_weight,
    residual,
    norm_gain,
    up_weight,
    head_weight,
):
    c = lax.axis_index("c")
    yl = lax.axis_index("yl")

    def rows_of(x, first, count):
        return lax.dynamic_slice_in_dim(x, first, count, 0)

    w10 = swap(out_weight, "xh")
    up_par = swap(up_weight, "c")
    w01 = swap(out_weight, "c")

    part = attend(
        queries,
        new_key,
        new_value,
        cache_keys,
        cache_values,
        lengths,
        prefix_keys,
        prefix_values,
        prompt_ids,
    )

    part = hold(part, up_par, w01)
    before, after = shift(part, 1), shift(part, 3)
    far = shift(before, 1)
    gain = jnp.broadcast_to(norm_gain[None, :], (16, 512))
    extra = swap(jnp.concatenate([rows_of(residual, (1 - c) * 128, 128), gain], axis=0), "c")
    res_y = swap(
        jnp.concatenate(
            [rows_of(residual, c * 128 + (1 - yl) * 64, 64), rows_of(extra, (1 - yl) * 64, 64)], axis=1
        ),
        "yl",
    )
    w10 = hold(w10, before, after)
    w11 = swap(w10, "c")

    weights = (out_weight, w01, w10, w11)
    partial = project((0, 1, 3), part, before, after, *weights)
    partial = project((2,), far, *weights, partial)
    parts = lax.all_to_all(partial, ("xh", "xl", "yh", "yl"), 0, 0, tiled=True)
    hid_mine, hid_par, sent = verify_up(parts, residual, extra, res_y, gain, up_weight, up_par)
    got = lax.all_to_all(sent.reshape(8, 16, 4096 + 128), ("z", "xh"), 0, 0, tiled=True)

    hid_back = swap(hid_par, "c")
    away = jnp.concatenate([rows_of(hid_mine, (1 - yl) * 64, 64), rows_of(hid_back, (1 - yl) * 64, 64)], axis=1)
    home = jnp.concatenate([rows_of(hid_mine, yl * 64, 64), rows_of(hid_back, yl * 64, 64)], axis=1)
    came = swap(away, "yl")
    block = jnp.where(
        yl == 0, jnp.concatenate([home, came], axis=0), jnp.concatenate([came, home], axis=0)
    )
    mine, back = block[:, :512], block[:, 512:]
    hidden = jnp.where(
        c == 0, jnp.concatenate([mine, back], axis=0), jnp.concatenate([back, mine], axis=0)
    )

    line = score(got, head_weight, prompt_ids, cluster_ids)
    scores, votes = tally(lax.all_to_all(line, AXES, 0, 0, tiled=True))
    return hidden, scores.reshape(256), votes.T


def solution(mesh):
    fine = Mesh(mesh.devices.reshape(4, 2, 2, 2, 2, 2), AXES)
    placed = (
        P(DP, TP),
        P(DP, TP),
        P(DP, TP),
        P(DP, TP, None, None),
        P(DP, TP, None, None),
        P(DP),
        P(DP, TP, None, None),
        P(DP, TP, None, None),
        P(DP),
        P(DP),
        P(TP, DP),
        P(TP, DP),
        P(DP),
        P(DP, None),
        P(),
    )
    return jax.shard_map(
        body,
        mesh=fine,
        in_specs=placed,
        out_specs=(P(TP, DP), P(TP), P()),
        check_vma=False,
    )
```

```python
import functools
import math

import jax
import jax.numpy as jnp
from jax import lax
from jax.experimental import pallas as pl
from jax.experimental.pallas import tpu as pltpu
from jax.sharding import Mesh, PartitionSpec as P

D = 8192
CLUSTERS = 16
PROMPTS_DEV = 2
eps = 1e-05
AXES = ("z", "xh", "c", "xl", "yh", "yl")
DP = ("z", "xh", "c")
TP = ("xl", "yh", "yl")
BF = jnp.bfloat16
F32 = jnp.float32
SCALE2 = math.log2(math.e) / math.sqrt(128)
NEG = -1e30
LIMIT = 63 * 1024 * 1024
NT = (((1,), (1,)), ((), ()))


def attn_kernel(rows, tile, ids_hbm, ids2_hbm, lens_hbm, q_hbm, nk_hbm, nv_hbm, pk_hbm, pv_hbm, ck_hbm, cv_hbm,
                out_ref, ids_s, ids_v, lens_v, q_ref, nk_ref, nv_ref, pk, pv, ck, cv, qs, nks, nvs, lens, acc,
                mbuf, lbuf, s_scr, sem_i, sem_p, sem_k, sem_v):
    small = [pltpu.make_async_copy(h, v, sem_i.at[i]) for i, (h, v) in enumerate((
        (ids_hbm, ids_s), (ids2_hbm, ids_v), (lens_hbm, lens_v), (q_hbm, q_ref), (nk_hbm, nk_ref), (nv_hbm, nv_ref)))]
    for cp in small:
        cp.start()
    heads = q_ref.shape[1] // 128
    tiles = rows // tile
    ctile = 16
    ctiles = rows // ctile
    keys = pk.shape[1]
    pre = [pltpu.make_async_copy(h.at[p], v.at[p], sem_p.at[p, i])
           for p in range(2) for i, (h, v) in enumerate(((pk_hbm, pk), (pv_hbm, pv)))]
    for cp in pre:
        cp.start()

    small[0].wait()

    def place(r, counts):
        c0, c1 = counts
        p = ids_s[r] & 1
        to = jnp.where(p == 0, c0, rows - 1 - c1)
        blk = to // ctile
        pltpu.make_async_copy(ck_hbm.at[r], ck.at[to], sem_k.at[blk]).start()
        pltpu.make_async_copy(cv_hbm.at[r], cv.at[to], sem_v.at[blk]).start()
        return c0 + 1 - p, c1 + p

    n0, _ = lax.fori_loop(0, rows, place, (jnp.int32(0), jnp.int32(0)), unroll=8)

    for cp in small[1:]:
        cp.wait()
    second = (ids_v[...] & 1)
    ones = jnp.broadcast_to(second, (rows, rows)).astype(F32).astype(BF)
    ri = lax.broadcasted_iota(jnp.int32, (rows, rows), 0)
    ci = lax.broadcasted_iota(jnp.int32, (rows, rows), 1)
    upper = (ri < ci).astype(F32).astype(BF)
    before1 = jnp.dot(ones, upper, preferred_element_type=F32)
    pos = jnp.where(jnp.broadcast_to(second, (rows, rows)) == 0, ci.astype(F32) - before1, rows - 1 - before1)
    perm32 = (pos == ri.astype(F32)).astype(F32)
    perm = perm32.astype(BF)
    unperm = perm32.T.astype(BF)
    qs[...] = jnp.dot(perm, q_ref[...], preferred_element_type=F32).astype(BF)
    nks[...] = jnp.dot(perm, nk_ref[...], preferred_element_type=F32)
    nvs[...] = jnp.dot(perm, nv_ref[...], preferred_element_type=F32)
    lb = jnp.broadcast_to(lens_v[...], (128, rows)).astype(F32).astype(BF)
    lens[...] = lax.dot_general(perm, lb, NT, preferred_element_type=F32)

    for cp in pre:
        cp.wait()
    edge = jnp.minimum(n0 // tile, tiles - 1)
    chunk = 512

    def prefix(item, _):
        p = (item > edge).astype(jnp.int32)
        row0 = pl.multiple_of((item - p) * tile, tile)
        qt = jnp.concatenate([qs[pl.ds(row0, tile), h * 128:(h + 1) * 128] for h in range(heads)], axis=0)
        top = None
        for k in range(0, keys, chunk):
            s = lax.dot_general(qt, pk[p, k:k + chunk], NT, preferred_element_type=F32)
            s_scr[:, k:k + chunk] = s
            for j in range(0, chunk, 128):
                top = s[:, j:j + 128] if top is None else jnp.maximum(top, s[:, j:j + 128])
        m = jnp.max(top, axis=1, keepdims=True)
        mb = jnp.broadcast_to(m, (heads * tile, 128))
        l = jnp.zeros((heads * tile, 128), F32)
        o = jnp.zeros((heads * tile, 128), F32)
        for k in range(0, keys, chunk):
            ps = []
            for j in range(0, chunk, 128):
                e = jnp.exp2((s_scr[:, k + j:k + j + 128] - mb) * SCALE2)
                l = l + e
                ps.append(e.astype(BF))
            o = o + jnp.dot(jnp.concatenate(ps, axis=1), pv[p, k:k + chunk], preferred_element_type=F32)
        lsum = jnp.broadcast_to(jnp.sum(l, axis=1, keepdims=True), (heads * tile, 128))
        at = row0 + lax.broadcasted_iota(jnp.int32, (tile, 128), 0)
        mine = (at < n0) == (p == 0)
        for h in range(heads):
            hs = slice(h * tile, (h + 1) * tile)
            cs = slice(h * 128, (h + 1) * 128)
            rs = pl.ds(row0, tile)
            acc[rs, cs] = jnp.where(mine, o[hs], acc[rs, cs])
            mbuf[rs, cs] = jnp.where(mine, mb[hs], mbuf[rs, cs])
            lbuf[rs, cs] = jnp.where(mine, lsum[hs], lbuf[rs, cs])
        return 0

    lax.fori_loop(0, tiles + 1, prefix, 0)

    mrow = lax.broadcasted_iota(jnp.int32, (heads * ctile, 128), 0) % ctile
    lane = lax.broadcasted_iota(jnp.int32, (heads * ctile, 128), 1).astype(F32)

    def cached(b, _):
        r0 = pl.multiple_of(b * ctile, ctile)
        rs = pl.ds(r0, ctile)
        pltpu.make_async_copy(ck_hbm.at[pl.ds(0, ctile)], ck.at[rs], sem_k.at[b]).wait()
        pltpu.make_async_copy(cv_hbm.at[pl.ds(0, ctile)], cv.at[rs], sem_v.at[b]).wait()
        heads_of = lambda ref: jnp.concatenate([ref[rs, h * 128:(h + 1) * 128] for h in range(heads)], axis=0)
        rep = lambda x: jnp.concatenate([x] * heads, axis=0)
        qt = heads_of(qs)
        kt = ck[rs].reshape(ctile * 128, 128)
        vt = cv[rs].reshape(ctile * 128, 128)
        s = lax.dot_general(qt, kt, NT, preferred_element_type=F32)
        sc = s[:, :128]
        for r in range(1, ctile):
            sc = jnp.where(mrow == r, s[:, r * 128:(r + 1) * 128], sc)
        sc = jnp.where(lane < rep(lens[rs]), sc, NEG)
        so = jnp.sum(qt.astype(F32) * rep(nks[rs]), axis=1, keepdims=True)
        mp = heads_of(mbuf)
        m = jnp.maximum(jnp.maximum(mp, jnp.max(sc, axis=1, keepdims=True)), so)
        ap = jnp.exp2((mp - m) * SCALE2)
        e = jnp.exp2((sc - m) * SCALE2)
        eo = jnp.exp2((so - m) * SCALE2)
        eb = e.astype(BF).astype(F32)
        pe = jnp.concatenate([jnp.where(mrow == r, eb, 0.0).astype(BF) for r in range(ctile)], axis=1)
        oc = jnp.dot(pe, vt, preferred_element_type=F32)
        l = ap * heads_of(lbuf) + jnp.sum(e, axis=1, keepdims=True) + eo
        o = (ap * heads_of(acc) + oc + eo * rep(nvs[rs])) / l
        for h in range(heads):
            qs[rs, h * 128:(h + 1) * 128] = o[h * ctile:(h + 1) * ctile].astype(BF)
        return 0

    lax.fori_loop(0, ctiles, cached, 0)
    out_ref[...] = jnp.dot(unperm, qs[...], preferred_element_type=F32).astype(BF)


def attend(queries, new_key, new_value, ck, cv, lengths, pk, pv, prompt_ids, tile=32):
    rows = queries.shape[0]
    width = queries.shape[1]
    keys = pk.shape[2]
    heads = width // 128
    V = pl.BlockSpec(memory_space=pltpu.VMEM)
    A = pl.BlockSpec(memory_space=pl.ANY)
    S = pl.BlockSpec(memory_space=pltpu.SMEM)
    return pl.pallas_call(
        functools.partial(attn_kernel, rows, tile),
        out_shape=jax.ShapeDtypeStruct((rows, width), BF),
        in_specs=[A] * 10,
        out_specs=V,
        scratch_shapes=[
            pltpu.SMEM((rows,), jnp.int32), pltpu.VMEM((1, rows), jnp.int32), pltpu.VMEM((1, rows), jnp.int32),
            pltpu.VMEM((rows, width), BF), pltpu.VMEM((rows, 128), BF), pltpu.VMEM((rows, 128), BF),
            pltpu.VMEM((2, keys, 128), BF), pltpu.VMEM((2, keys, 128), BF),
            pltpu.VMEM((rows, 128, 128), BF), pltpu.VMEM((rows, 128, 128), BF),
            pltpu.VMEM((rows, width), BF), pltpu.VMEM((rows, 128), F32), pltpu.VMEM((rows, 128), F32),
            pltpu.VMEM((rows, 128), F32),
            pltpu.VMEM((rows, width), F32), pltpu.VMEM((rows, width), F32), pltpu.VMEM((rows, width), F32),
            pltpu.VMEM((heads * tile, keys), F32),
            pltpu.SemaphoreType.DMA((6,)), pltpu.SemaphoreType.DMA((2, 2)), pltpu.SemaphoreType.DMA((rows // 16,)), pltpu.SemaphoreType.DMA((rows // 16,)),
        ],
        compiler_params=pltpu.CompilerParams(vmem_limit_bytes=LIMIT),
        cost_estimate=pl.CostEstimate(flops=16 * 10**9, bytes_accessed=11 * 1024 * 1024, transcendentals=2 * 1024 * 1024),
    )(prompt_ids, prompt_ids.reshape(1, rows), lengths.reshape(1, rows), queries, new_key, new_value,
      pk.reshape(2, keys, 128), pv.reshape(2, keys, 128), ck.reshape(rows, 128, 128), cv.reshape(rows, 128, 128))


def swap(x, axis):
    return lax.ppermute(x, axis, [(0, 1), (1, 0)])


def shift(x, by):
    return lax.ppermute(x, "z", [(i, (i + by) % 4) for i in range(4)])


def tiny(mib, flops=1024, **kw):
    return dict(
        compiler_params=pltpu.CompilerParams(vmem_limit_bytes=mib * 1024 * 1024),
        cost_estimate=pl.CostEstimate(flops=flops, bytes_accessed=1024, transcendentals=0),
        **kw,
    )


def hold_kernel(*refs):
    pass


def hold(x, *tokens, mib=4):
    A = pl.BlockSpec(memory_space=pl.ANY)
    return pl.pallas_call(
        hold_kernel,
        out_shape=jax.ShapeDtypeStruct(x.shape, x.dtype),
        in_specs=[A] * (1 + len(tokens)),
        out_specs=A,
        input_output_aliases={0: 0},
        **tiny(mib),
    )(x, *tokens)


def proj_kernel(steps, *refs):
    count = len(steps)
    rows, weights = refs[:count], refs[count : count + 4]
    out, w, chunks, sems = refs[-4:]
    loads = [
        pltpu.make_async_copy(src, w.at[:, j * 512 : (j + 1) * 512], sems.at[j])
        for j, src in enumerate(weights)
    ]
    for load in loads:
        load.start()
    a = jnp.concatenate([row[...] for row in rows], axis=0)
    z = lax.axis_index("z")
    xh = lax.axis_index("xh")
    leave = []
    for j in range(4):
        loads[j].wait()
        total = jnp.dot(a, w[:, j * 512 : (j + 1) * 512], preferred_element_type=F32).astype(BF)
        total = total.reshape(count, 2, 64, 512)
        for i in range(count):
            chunks[j // 2, i, :, :, (j % 2) * 512 : (j % 2 + 1) * 512] = total[i]
        if j % 2:
            for i, step in enumerate(steps):
                first = ((xh ^ (j // 2)) * 4 + ((z - step) & 3)) * 2
                leave.append(
                    pltpu.make_async_copy(chunks.at[j // 2, i], out.at[pl.ds(first, 2)], sems.at[4 + j // 2 * count + i])
                )
                leave[-1].start()
    for copy in leave:
        copy.wait()


def project(steps, *ins):
    count = len(steps)
    more = len(ins) > count + 4
    V = pl.BlockSpec(memory_space=pltpu.VMEM)
    A = pl.BlockSpec(memory_space=pl.ANY)
    return pl.pallas_call(
        functools.partial(proj_kernel, steps),
        out_shape=jax.ShapeDtypeStruct((16, 64, 1024), BF),
        in_specs=[V] * count + [A] * (len(ins) - count),
        out_specs=A,
        input_output_aliases={count + 4: 0} if more else {},
        scratch_shapes=[
            pltpu.VMEM((1024, 2048), BF),
            pltpu.VMEM((2, count, 2, 64, 1024), BF),
            pltpu.SemaphoreType.DMA((4 + 2 * count,)),
        ],
        **tiny(48, 0),
    )(*ins)


def up_kernel(
    parts, res, extra, res_y, gain, gain_par, up_mine, up_par,
    hm_ref, hp_ref, sent_ref, parts_v, res_v, gain_v, gain2_v, w, sems,
):
    c = lax.axis_index("c")
    yl = lax.axis_index("yl")
    here = pl.ds(pl.multiple_of(yl * 64, 64), 64)
    there = pl.ds(pl.multiple_of(64 - yl * 64, 64), 64)
    small = [
        pltpu.make_async_copy(src, dst, sems.at[i // 4, i % 4])
        for i, (src, dst) in enumerate((
            (parts.at[:8], parts_v.at[:8]), (parts.at[8:], parts_v.at[8:]),
            (res.at[pl.ds(pl.multiple_of(c * 128 + yl * 64, 64), 64)], res_v.at[here, :512]),
            (extra.at[here], res_v.at[here, 512:]),
            (res_y, res_v.at[there]),
            (gain, gain_v), (gain_par, gain2_v),
        ))
    ]
    for copy in small:
        copy.start()
    loads = []
    for j in range(4):
        cols = slice(j * 1024, (j + 1) * 1024)
        loads.append((
            pltpu.make_async_copy(up_mine.at[:, cols], w.at[0:512, cols], sems.at[2, j]),
            pltpu.make_async_copy(up_par.at[:, cols], w.at[512:1024, cols], sems.at[3, j]),
        ))
        for load in loads[-1]:
            load.start()
    for copy in small:
        copy.wait()

    def summed(first):
        total = parts_v[first].astype(F32)
        for i in range(1, 8):
            total = total + parts_v[first + i].astype(F32)
        return total

    mixed = jnp.concatenate([summed(0), summed(8)], axis=0)
    hid = (res_v[...].astype(F32) + mixed).astype(BF)
    hm_ref[...] = hid[:, :512]
    hp_ref[...] = hid[:, 512:]
    wide = hid.astype(F32)
    squares = jnp.sum(wide * wide, axis=1, keepdims=True)
    hi = squares.astype(BF).astype(F32)
    lane = lax.broadcasted_iota(jnp.int32, (128, 128), 1)
    sent_ref[:, 4096:] = jnp.where(lane == 0, hi, jnp.where(lane == 1, squares - hi, 0.0)).astype(BF)
    gains = jnp.concatenate([gain_v[0:1], gain2_v[0:1]], axis=1).astype(F32)
    gained = (wide * gains).astype(BF)
    for j in range(4):
        cols = slice(j * 1024, (j + 1) * 1024)
        for load in loads[j]:
            load.wait()
        sent_ref[:, cols] = jnp.dot(gained, w[:, cols], preferred_element_type=F32).astype(BF)


def verify_up(*ins):
    V = pl.BlockSpec(memory_space=pltpu.VMEM)
    A = pl.BlockSpec(memory_space=pl.ANY)
    return pl.pallas_call(
        up_kernel,
        out_shape=(
            jax.ShapeDtypeStruct((128, 512), BF),
            jax.ShapeDtypeStruct((128, 512), BF),
            jax.ShapeDtypeStruct((128, 4096 + 128), BF),
        ),
        in_specs=[A] * 8,
        out_specs=(V, V, V),
        scratch_shapes=[
            pltpu.VMEM((16, 64, 1024), BF),
            pltpu.VMEM((128, 1024), BF),
            pltpu.VMEM((16, 512), BF),
            pltpu.VMEM((16, 512), BF),
            pltpu.VMEM((1024, 4096), BF),
            pltpu.SemaphoreType.DMA((4, 4)),
        ],
        **tiny(48),
    )(*ins)


def score_kernel(got_hbm, head_hbm, prompts_hbm, clusters_hbm, out_ref, got, head, prompts, clusters, sems):
    copies = [
        pltpu.make_async_copy(src, dst, sems.at[i])
        for i, (src, dst) in enumerate((
            (got_hbm, got), (head_hbm, head), (prompts_hbm, prompts), (clusters_hbm, clusters)
        ))
    ]
    for copy in copies:
        copy.start()
    for copy in copies:
        copy.wait()

    def summed(cols):
        total = got[0, :, cols].astype(F32)
        for i in range(1, 8):
            total = total + got[i, :, cols].astype(F32)
        return total

    tail = summed(slice(4096, 4224))
    squares = tail[:, 0:1] + tail[:, 1:2]
    factor = lax.rsqrt(squares / D + eps)
    acc = jnp.zeros((16, 512), F32)
    for j in range(0, 4096, 512):
        cols = slice(j, j + 512)
        up = summed(cols) * factor
        acc = acc + up / (1.0 + jnp.exp(-up)) * head[0:1, cols].astype(F32)
    scores = jnp.sum(acc, axis=1, keepdims=True)
    row = lax.broadcasted_iota(jnp.int32, (16, 128), 0)
    lane = lax.broadcasted_iota(jnp.int32, (16, 128), 1)
    line = jnp.sum(jnp.where(row == lane, scores, 0.0), axis=0, keepdims=True)
    pair = ((prompts[...] & 1) * CLUSTERS + clusters[...]).astype(F32)
    t = lax.axis_index(TP)
    pair = pltpu.roll(jnp.broadcast_to(pair, (8, 128)), (144 - t * 16) & 127, 1)[0:1]
    lane = lane[0:1]
    mine = jnp.where(lane < 16, line, jnp.where(lane < 32, pair, 0.0))
    out_ref[...] = jnp.broadcast_to(mine.reshape(1, 1, 128), (128, 1, 128))


def score(got, head_weight, prompt_ids, cluster_ids):
    V = pl.BlockSpec(memory_space=pltpu.VMEM)
    A = pl.BlockSpec(memory_space=pl.ANY)
    return pl.pallas_call(
        score_kernel,
        out_shape=jax.ShapeDtypeStruct((128, 1, 128), F32),
        in_specs=[A] * 4,
        out_specs=V,
        scratch_shapes=[
            pltpu.VMEM((8, 16, 4096 + 128), BF),
            pltpu.VMEM((1, 4096), BF),
            pltpu.VMEM((1, 128), jnp.int32),
            pltpu.VMEM((1, 128), jnp.int32),
            pltpu.SemaphoreType.DMA((4,)),
        ],
        **tiny(40),
    )(got, head_weight.reshape(1, 4096), prompt_ids.reshape(1, 128), cluster_ids.reshape(1, 128))


def vote_kernel(all_hbm, scores_ref, votes_ref, x3, x, vals, ids, votes, sem):
    copy = pltpu.make_async_copy(all_hbm, x3, sem)
    copy.start()
    copy.wait()
    x[...] = x3[...].reshape(128, 128)
    t = lax.axis_index(TP)
    lane8 = lax.broadcasted_iota(jnp.int32, (8, 128), 1)
    row8 = lax.broadcasted_iota(jnp.int32, (8, 128), 0)
    lane = lax.broadcasted_iota(jnp.int32, (16, 128), 1)
    place = lane8 // 16 == row8

    def line(block, first):
        front = pltpu.roll(block, 128 - first, 1) if first else block
        rolled = pltpu.roll(front, 0, 1, stride=16, stride_axis=0)
        return jnp.sum(jnp.where(place, rolled, 0.0), axis=0, keepdims=True)

    def scores_of(zx, c):
        base = (zx & 1) * 64 + c * 8 + (zx >> 1) * 2
        return jnp.concatenate(
            [x[pl.ds(base, 4, stride=16), :], x[pl.ds(base + 1, 4, stride=16), :]], axis=0
        )

    for c in range(2):
        scores_ref[c : c + 1, :] = line(scores_of(t, c), 0)
    for zx in range(8):
        for c in range(2):
            dp = zx * 2 + c
            vals[dp : dp + 1, :] = line(scores_of(zx, c), 0)
            ids[dp : dp + 1, :] = line(x[dp * 8 : dp * 8 + 8, :], 16)
    votes[...] = jnp.zeros((128, 128), F32)
    for p in range(2):
        acc = jnp.zeros((16, 128), F32)
        for k in range(CLUSTERS):
            hit = jnp.where(ids[...] == float(p * CLUSTERS + k), vals[...], 0.0)
            acc = jnp.where(lane == k, jnp.sum(hit, axis=1, keepdims=True), acc)
        votes[pl.ds(p, 16, stride=2), :] = acc
    votes_ref[...] = votes[...].T[:CLUSTERS, :32]


def tally(everyone):
    V = pl.BlockSpec(memory_space=pltpu.VMEM)
    A = pl.BlockSpec(memory_space=pl.ANY)
    return pl.pallas_call(
        vote_kernel,
        out_shape=(jax.ShapeDtypeStruct((2, 128), F32), jax.ShapeDtypeStruct((CLUSTERS, 32), F32)),
        in_specs=[A],
        out_specs=(V, V),
        scratch_shapes=[
            pltpu.VMEM((128, 1, 128), F32),
            pltpu.VMEM((128, 128), F32),
            pltpu.VMEM((16, 128), F32),
            pltpu.VMEM((16, 128), F32),
            pltpu.VMEM((128, 128), F32),
            pltpu.SemaphoreType.DMA,
        ],
        **tiny(40),
    )(everyone)


def body(
    queries,
    new_key,
    new_value,
    cache_keys,
    cache_values,
    lengths,
    prefix_keys,
    prefix_values,
    prompt_ids,
    cluster_ids,
    out_weight,
    residual,
    norm_gain,
    up_weight,
    head_weight,
):
    c = lax.axis_index("c")
    yl = lax.axis_index("yl")

    def rows_of(x, first, count):
        return lax.dynamic_slice_in_dim(x, first, count, 0)

    w10 = swap(out_weight, "xh")
    up_par = swap(up_weight, "c")
    w01 = swap(out_weight, "c")

    part = attend(
        queries,
        new_key,
        new_value,
        cache_keys,
        cache_values,
        lengths,
        prefix_keys,
        prefix_values,
        prompt_ids,
    )

    part = hold(part, up_par, w01, mib=63)
    before, after = shift(part, 1), shift(part, 3)
    far = shift(before, 1)
    gain = jnp.broadcast_to(norm_gain[None, :], (16, 512))
    gain_par = swap(gain, "c")
    later = hold(residual, part)
    extra = swap(rows_of(later, (1 - c) * 128, 128), "c")
    res_y = swap(
        jnp.concatenate(
            [rows_of(later, c * 128 + (1 - yl) * 64, 64), rows_of(extra, (1 - yl) * 64, 64)], axis=1
        ),
        "yl",
    )
    w10 = hold(w10, before, after, res_y)
    w11 = swap(w10, "c")

    weights = (out_weight, w01, w10, w11)
    partial = project((0, 1, 3), part, before, after, *weights)
    partial = project((2,), far, *weights, partial)
    parts = lax.all_to_all(partial, ("xh", "xl", "yh", "yl"), 0, 0, tiled=True)
    hid_mine, hid_par, sent = verify_up(parts, residual, extra, res_y, gain, gain_par, up_weight, up_par)
    got = lax.all_to_all(sent.reshape(8, 16, 4096 + 128), ("z", "xh"), 0, 0, tiled=True)

    hid_back = swap(hid_par, "c")
    away = jnp.concatenate([rows_of(hid_mine, (1 - yl) * 64, 64), rows_of(hid_back, (1 - yl) * 64, 64)], axis=1)
    home = jnp.concatenate([rows_of(hid_mine, yl * 64, 64), rows_of(hid_back, yl * 64, 64)], axis=1)
    came = swap(away, "yl")
    block = jnp.where(
        yl == 0, jnp.concatenate([home, came], axis=0), jnp.concatenate([came, home], axis=0)
    )
    mine, back = block[:, :512], block[:, 512:]
    hidden = jnp.where(
        c == 0, jnp.concatenate([mine, back], axis=0), jnp.concatenate([back, mine], axis=0)
    )

    line = score(got, head_weight, prompt_ids, cluster_ids)
    scores, votes = tally(lax.all_to_all(line, AXES, 0, 0, tiled=True))
    return hidden, scores.reshape(256), votes.T


def solution(mesh):
    fine = Mesh(mesh.devices.reshape(4, 2, 2, 2, 2, 2), AXES)
    placed = (
        P(DP, TP),
        P(DP, TP),
        P(DP, TP),
        P(DP, TP, None, None),
        P(DP, TP, None, None),
        P(DP),
        P(DP, TP, None, None),
        P(DP, TP, None, None),
        P(DP),
        P(DP),
        P(TP, DP),
        P(TP, DP),
        P(DP),
        P(DP, None),
        P(),
    )
    return jax.shard_map(
        body,
        mesh=fine,
        in_specs=placed,
        out_specs=(P(TP, DP), P(TP), P()),
        check_vma=False,
    )
```

```python
import functools
import math

import jax
import jax.numpy as jnp
from jax import lax
from jax.experimental import pallas as pl
from jax.experimental.pallas import tpu as pltpu
from jax.sharding import Mesh, PartitionSpec as P

D = 8192
CLUSTERS = 16
PROMPTS_DEV = 2
eps = 1e-05
AXES = ("z", "xh", "c", "xl", "yh", "yl")
DP = ("z", "xh", "c")
TP = ("xl", "yh", "yl")
BF = jnp.bfloat16
F32 = jnp.float32
SCALE2 = math.log2(math.e) / math.sqrt(128)
NEG = -1e30
LIMIT = 63 * 1024 * 1024
NT = (((1,), (1,)), ((), ()))


def attn_kernel(rows, tile, ids_hbm, ids2_hbm, lens_hbm, q_hbm, nk_hbm, nv_hbm, pk_hbm, pv_hbm, ck_hbm, cv_hbm,
                out_ref, ids_s, ids_v, lens_v, q_ref, nk_ref, nv_ref, pk, pv, ck, cv, qs, nks, nvs, lens, acc,
                mbuf, lbuf, s_scr, sem_i, sem_p, sem_k, sem_v):
    small = [pltpu.make_async_copy(h, v, sem_i.at[i]) for i, (h, v) in enumerate((
        (ids_hbm, ids_s), (ids2_hbm, ids_v), (lens_hbm, lens_v), (q_hbm, q_ref), (nk_hbm, nk_ref), (nv_hbm, nv_ref)))]
    for cp in small:
        cp.start()
    heads = q_ref.shape[1] // 128
    tiles = rows // tile
    ctile = 16
    ctiles = rows // ctile
    keys = pk.shape[1]
    pre = [pltpu.make_async_copy(h.at[p], v.at[p], sem_p.at[p, i])
           for p in range(2) for i, (h, v) in enumerate(((pk_hbm, pk), (pv_hbm, pv)))]
    for cp in pre:
        cp.start()

    small[0].wait()

    def place(r, counts):
        c0, c1 = counts
        p = ids_s[r] & 1
        to = jnp.where(p == 0, c0, rows - 1 - c1)
        blk = to // ctile
        pltpu.make_async_copy(ck_hbm.at[r], ck.at[to], sem_k.at[blk]).start()
        pltpu.make_async_copy(cv_hbm.at[r], cv.at[to], sem_v.at[blk]).start()
        return c0 + 1 - p, c1 + p

    n0, _ = lax.fori_loop(0, rows, place, (jnp.int32(0), jnp.int32(0)), unroll=8)

    for cp in small[1:]:
        cp.wait()
    second = (ids_v[...] & 1)
    ones = jnp.broadcast_to(second, (rows, rows)).astype(F32).astype(BF)
    ri = lax.broadcasted_iota(jnp.int32, (rows, rows), 0)
    ci = lax.broadcasted_iota(jnp.int32, (rows, rows), 1)
    upper = (ri < ci).astype(F32).astype(BF)
    before1 = jnp.dot(ones, upper, preferred_element_type=F32)
    pos = jnp.where(jnp.broadcast_to(second, (rows, rows)) == 0, ci.astype(F32) - before1, rows - 1 - before1)
    perm32 = (pos == ri.astype(F32)).astype(F32)
    perm = perm32.astype(BF)
    unperm = perm32.T.astype(BF)
    qs[...] = jnp.dot(perm, q_ref[...], preferred_element_type=F32).astype(BF)
    nks[...] = jnp.dot(perm, nk_ref[...], preferred_element_type=F32)
    nvs[...] = jnp.dot(perm, nv_ref[...], preferred_element_type=F32)
    lb = jnp.broadcast_to(lens_v[...], (128, rows)).astype(F32).astype(BF)
    lens[...] = lax.dot_general(perm, lb, NT, preferred_element_type=F32)

    for cp in pre:
        cp.wait()
    edge = jnp.minimum(n0 // tile, tiles - 1)
    chunk = 512

    def prefix(item, _):
        p = (item > edge).astype(jnp.int32)
        row0 = pl.multiple_of((item - p) * tile, tile)
        qt = jnp.concatenate([qs[pl.ds(row0, tile), h * 128:(h + 1) * 128] for h in range(heads)], axis=0)
        top = None
        for k in range(0, keys, chunk):
            s = lax.dot_general(qt, pk[p, k:k + chunk], NT, preferred_element_type=F32)
            s_scr[:, k:k + chunk] = s
            for j in range(0, chunk, 128):
                top = s[:, j:j + 128] if top is None else jnp.maximum(top, s[:, j:j + 128])
        m = jnp.max(top, axis=1, keepdims=True)
        mb = jnp.broadcast_to(m, (heads * tile, 128))
        l = jnp.zeros((heads * tile, 128), F32)
        o = jnp.zeros((heads * tile, 128), F32)
        for k in range(0, keys, chunk):
            ps = []
            for j in range(0, chunk, 128):
                e = jnp.exp2((s_scr[:, k + j:k + j + 128] - mb) * SCALE2)
                l = l + e
                ps.append(e.astype(BF))
            o = o + jnp.dot(jnp.concatenate(ps, axis=1), pv[p, k:k + chunk], preferred_element_type=F32)
        lsum = jnp.broadcast_to(jnp.sum(l, axis=1, keepdims=True), (heads * tile, 128))
        at = row0 + lax.broadcasted_iota(jnp.int32, (tile, 128), 0)
        mine = (at < n0) == (p == 0)
        for h in range(heads):
            hs = slice(h * tile, (h + 1) * tile)
            cs = slice(h * 128, (h + 1) * 128)
            rs = pl.ds(row0, tile)
            acc[rs, cs] = jnp.where(mine, o[hs], acc[rs, cs])
            mbuf[rs, cs] = jnp.where(mine, mb[hs], mbuf[rs, cs])
            lbuf[rs, cs] = jnp.where(mine, lsum[hs], lbuf[rs, cs])
        return 0

    lax.fori_loop(0, tiles + 1, prefix, 0)

    mrow = lax.broadcasted_iota(jnp.int32, (heads * ctile, 128), 0) % ctile
    lane = lax.broadcasted_iota(jnp.int32, (heads * ctile, 128), 1).astype(F32)

    def cached(b, _):
        r0 = pl.multiple_of(b * ctile, ctile)
        rs = pl.ds(r0, ctile)
        pltpu.make_async_copy(ck_hbm.at[pl.ds(0, ctile)], ck.at[rs], sem_k.at[b]).wait()
        pltpu.make_async_copy(cv_hbm.at[pl.ds(0, ctile)], cv.at[rs], sem_v.at[b]).wait()
        heads_of = lambda ref: jnp.concatenate([ref[rs, h * 128:(h + 1) * 128] for h in range(heads)], axis=0)
        rep = lambda x: jnp.concatenate([x] * heads, axis=0)
        qt = heads_of(qs)
        kt = ck[rs].reshape(ctile * 128, 128)
        vt = cv[rs].reshape(ctile * 128, 128)
        s = lax.dot_general(qt, kt, NT, preferred_element_type=F32)
        sc = s[:, :128]
        for r in range(1, ctile):
            sc = jnp.where(mrow == r, s[:, r * 128:(r + 1) * 128], sc)
        sc = jnp.where(lane < rep(lens[rs]), sc, NEG)
        so = jnp.sum(qt.astype(F32) * rep(nks[rs]), axis=1, keepdims=True)
        mp = heads_of(mbuf)
        m = jnp.maximum(jnp.maximum(mp, jnp.max(sc, axis=1, keepdims=True)), so)
        ap = jnp.exp2((mp - m) * SCALE2)
        e = jnp.exp2((sc - m) * SCALE2)
        eo = jnp.exp2((so - m) * SCALE2)
        eb = e.astype(BF).astype(F32)
        pe = jnp.concatenate([jnp.where(mrow == r, eb, 0.0).astype(BF) for r in range(ctile)], axis=1)
        oc = jnp.dot(pe, vt, preferred_element_type=F32)
        l = ap * heads_of(lbuf) + jnp.sum(e, axis=1, keepdims=True) + eo
        o = (ap * heads_of(acc) + oc + eo * rep(nvs[rs])) / l
        for h in range(heads):
            qs[rs, h * 128:(h + 1) * 128] = o[h * ctile:(h + 1) * ctile].astype(BF)
        return 0

    lax.fori_loop(0, ctiles, cached, 0)
    out_ref[...] = jnp.dot(unperm, qs[...], preferred_element_type=F32).astype(BF)


def attend(queries, new_key, new_value, ck, cv, lengths, pk, pv, prompt_ids, tile=32):
    rows = queries.shape[0]
    width = queries.shape[1]
    keys = pk.shape[2]
    heads = width // 128
    V = pl.BlockSpec(memory_space=pltpu.VMEM)
    A = pl.BlockSpec(memory_space=pl.ANY)
    S = pl.BlockSpec(memory_space=pltpu.SMEM)
    return pl.pallas_call(
        functools.partial(attn_kernel, rows, tile),
        out_shape=jax.ShapeDtypeStruct((rows, width), BF),
        in_specs=[A] * 10,
        out_specs=V,
        scratch_shapes=[
            pltpu.SMEM((rows,), jnp.int32), pltpu.VMEM((1, rows), jnp.int32), pltpu.VMEM((1, rows), jnp.int32),
            pltpu.VMEM((rows, width), BF), pltpu.VMEM((rows, 128), BF), pltpu.VMEM((rows, 128), BF),
            pltpu.VMEM((2, keys, 128), BF), pltpu.VMEM((2, keys, 128), BF),
            pltpu.VMEM((rows, 128, 128), BF), pltpu.VMEM((rows, 128, 128), BF),
            pltpu.VMEM((rows, width), BF), pltpu.VMEM((rows, 128), F32), pltpu.VMEM((rows, 128), F32),
            pltpu.VMEM((rows, 128), F32),
            pltpu.VMEM((rows, width), F32), pltpu.VMEM((rows, width), F32), pltpu.VMEM((rows, width), F32),
            pltpu.VMEM((heads * tile, keys), F32),
            pltpu.SemaphoreType.DMA((6,)), pltpu.SemaphoreType.DMA((2, 2)), pltpu.SemaphoreType.DMA((rows // 16,)), pltpu.SemaphoreType.DMA((rows // 16,)),
        ],
        compiler_params=pltpu.CompilerParams(vmem_limit_bytes=LIMIT),
        cost_estimate=pl.CostEstimate(flops=16 * 10**9, bytes_accessed=11 * 1024 * 1024, transcendentals=2 * 1024 * 1024),
    )(prompt_ids, prompt_ids.reshape(1, rows), lengths.reshape(1, rows), queries, new_key, new_value,
      pk.reshape(2, keys, 128), pv.reshape(2, keys, 128), ck.reshape(rows, 128, 128), cv.reshape(rows, 128, 128))


def swap(x, axis):
    return lax.ppermute(x, axis, [(0, 1), (1, 0)])


def shift(x, by):
    return lax.ppermute(x, "z", [(i, (i + by) % 4) for i in range(4)])


def tiny(mib, flops=1024, **kw):
    return dict(
        compiler_params=pltpu.CompilerParams(vmem_limit_bytes=mib * 1024 * 1024),
        cost_estimate=pl.CostEstimate(flops=flops, bytes_accessed=1024, transcendentals=0),
        **kw,
    )


def hold_kernel(*refs):
    pass


def hold(x, *tokens, mib=4):
    A = pl.BlockSpec(memory_space=pl.ANY)
    return pl.pallas_call(
        hold_kernel,
        out_shape=jax.ShapeDtypeStruct(x.shape, x.dtype),
        in_specs=[A] * (1 + len(tokens)),
        out_specs=A,
        input_output_aliases={0: 0},
        **tiny(mib),
    )(x, *tokens)


def proj_kernel(steps, *refs):
    count = len(steps)
    given = len(refs) - 8 - (count == 1)
    rows, weights = refs[:given], refs[given : given + 4]
    out, w, chunks, sems = refs[-4:]
    loads = [
        pltpu.make_async_copy(src, w.at[:, j * 512 : (j + 1) * 512], sems.at[j])
        for j, src in enumerate(weights)
    ]
    for load in loads:
        load.start()
    a = jnp.concatenate([row[...] for row in rows], axis=0)
    z = lax.axis_index("z")
    xh = lax.axis_index("xh")
    leave = []
    for j in range(4):
        loads[j].wait()
        total = jnp.dot(a, w[:, j * 512 : (j + 1) * 512], preferred_element_type=F32).astype(BF)
        total = total.reshape(count, 2, 64, 512)
        for i in range(count):
            chunks[j // 2, i, :, :, (j % 2) * 512 : (j % 2 + 1) * 512] = total[i]
        if j % 2:
            for i, step in enumerate(steps):
                first = ((xh ^ (j // 2)) * 4 + ((z - step) & 3)) * 2
                leave.append(
                    pltpu.make_async_copy(chunks.at[j // 2, i], out.at[pl.ds(first, 2)], sems.at[4 + j // 2 * count + i])
                )
                leave[-1].start()
    for copy in leave:
        copy.wait()


def project(steps, *ins):
    count = len(steps)
    more = count == 1
    given = len(ins) - 4 - more
    V = pl.BlockSpec(memory_space=pltpu.VMEM)
    A = pl.BlockSpec(memory_space=pl.ANY)
    return pl.pallas_call(
        functools.partial(proj_kernel, steps),
        out_shape=jax.ShapeDtypeStruct((16, 64, 1024), BF),
        in_specs=[V] * given + [A] * (len(ins) - given),
        out_specs=A,
        input_output_aliases={given + 4: 0} if more else {},
        scratch_shapes=[
            pltpu.VMEM((1024, 2048), BF),
            pltpu.VMEM((2, count, 2, 64, 1024), BF),
            pltpu.SemaphoreType.DMA((4 + 2 * count,)),
        ],
        **tiny(48, 0),
    )(*ins)


def up_kernel(
    parts, res, extra, res_y, gain, gain_par, up_mine, up_par,
    hm_ref, hp_ref, sent_ref, res_v, gain_v, gain2_v, w, sent, sems,
):
    c = lax.axis_index("c")
    yl = lax.axis_index("yl")
    here = pl.ds(pl.multiple_of(yl * 64, 64), 64)
    there = pl.ds(pl.multiple_of(64 - yl * 64, 64), 64)
    small = [
        pltpu.make_async_copy(src, dst, sems.at[i // 4, i % 4])
        for i, (src, dst) in enumerate((
            (res.at[pl.ds(pl.multiple_of(c * 128 + yl * 64, 64), 64)], res_v.at[here, :512]),
            (extra.at[here], res_v.at[here, 512:]),
            (res_y, res_v.at[there]),
            (gain, gain_v), (gain_par, gain2_v),
        ))
    ]
    loads = []
    for j in range(4):
        cols = slice(j * 1024, (j + 1) * 1024)
        loads.append((
            pltpu.make_async_copy(up_mine.at[:, cols], w.at[0:512, cols], sems.at[2, j]),
            pltpu.make_async_copy(up_par.at[:, cols], w.at[512:1024, cols], sems.at[3, j]),
        ))
        for load in loads[-1]:
            load.start()
        if j == 0:
            for copy in small:
                copy.start()
    for copy in small:
        copy.wait()

    def summed(first):
        total = parts[first].astype(F32)
        for i in range(1, 8):
            total = total + parts[first + i].astype(F32)
        return total

    mixed = jnp.concatenate([summed(0), summed(8)], axis=0)
    hid = (res_v[...].astype(F32) + mixed).astype(BF)
    hm_ref[...] = hid[:, :512]
    hp_ref[...] = hid[:, 512:]
    wide = hid.astype(F32)
    squares = jnp.sum(wide * wide, axis=1, keepdims=True)
    hi = squares.astype(BF).astype(F32)
    lane = lax.broadcasted_iota(jnp.int32, (128, 128), 1)
    sent[:, 4096:] = jnp.where(lane == 0, hi, jnp.where(lane == 1, squares - hi, 0.0)).astype(BF)
    gains = jnp.concatenate([gain_v[0:1], gain2_v[0:1]], axis=1).astype(F32)
    gained = (wide * gains).astype(BF)
    leave = []
    for j in range(4):
        cols = slice(j * 1024, (j + 1) * 1024)
        for load in loads[j]:
            load.wait()
        sent[:, cols] = jnp.dot(gained, w[:, cols], preferred_element_type=F32).astype(BF)
        out = slice(j * 1024, (j + 1) * 1024 + (128 if j == 3 else 0))
        leave.append(pltpu.make_async_copy(sent.at[:, out], sent_ref.at[:, out], sems.at[4, j]))
        leave[-1].start()
    for copy in leave:
        copy.wait()


def verify_up(*ins):
    V = pl.BlockSpec(memory_space=pltpu.VMEM)
    A = pl.BlockSpec(memory_space=pl.ANY)
    return pl.pallas_call(
        up_kernel,
        out_shape=(
            jax.ShapeDtypeStruct((128, 512), BF),
            jax.ShapeDtypeStruct((128, 512), BF),
            jax.ShapeDtypeStruct((128, 4096 + 128), BF),
        ),
        in_specs=[V] + [A] * 7,
        out_specs=(V, V, A),
        scratch_shapes=[
            pltpu.VMEM((128, 1024), BF),
            pltpu.VMEM((16, 512), BF),
            pltpu.VMEM((16, 512), BF),
            pltpu.VMEM((1024, 4096), BF),
            pltpu.VMEM((128, 4096 + 128), BF),
            pltpu.SemaphoreType.DMA((5, 4)),
        ],
        **tiny(48),
    )(*ins)


def score_kernel(got_hbm, head_hbm, prompts_hbm, clusters_hbm, out_ref, got, head, prompts, clusters, sems):
    copies = [
        pltpu.make_async_copy(src, dst, sems.at[i])
        for i, (src, dst) in enumerate((
            (got_hbm, got), (head_hbm, head), (prompts_hbm, prompts), (clusters_hbm, clusters)
        ))
    ]
    for copy in copies:
        copy.start()
    for copy in copies:
        copy.wait()

    def summed(cols):
        total = got[0, :, cols].astype(F32)
        for i in range(1, 8):
            total = total + got[i, :, cols].astype(F32)
        return total

    tail = summed(slice(4096, 4224))
    squares = tail[:, 0:1] + tail[:, 1:2]
    factor = lax.rsqrt(squares / D + eps)
    acc = jnp.zeros((16, 512), F32)
    for j in range(0, 4096, 512):
        cols = slice(j, j + 512)
        up = summed(cols) * factor
        acc = acc + up / (1.0 + jnp.exp(-up)) * head[0:1, cols].astype(F32)
    scores = jnp.sum(acc, axis=1, keepdims=True)
    row = lax.broadcasted_iota(jnp.int32, (16, 128), 0)
    lane = lax.broadcasted_iota(jnp.int32, (16, 128), 1)
    line = jnp.sum(jnp.where(row == lane, scores, 0.0), axis=0, keepdims=True)
    pair = ((prompts[...] & 1) * CLUSTERS + clusters[...]).astype(F32)
    t = lax.axis_index(TP)
    pair = pltpu.roll(jnp.broadcast_to(pair, (8, 128)), (144 - t * 16) & 127, 1)[0:1]
    lane = lane[0:1]
    mine = jnp.where(lane < 16, line, jnp.where(lane < 32, pair, 0.0))
    out_ref[...] = jnp.broadcast_to(mine.reshape(1, 1, 128), (128, 1, 128))


def score(got, head_weight, prompt_ids, cluster_ids):
    V = pl.BlockSpec(memory_space=pltpu.VMEM)
    A = pl.BlockSpec(memory_space=pl.ANY)
    return pl.pallas_call(
        score_kernel,
        out_shape=jax.ShapeDtypeStruct((128, 1, 128), F32),
        in_specs=[A] * 4,
        out_specs=V,
        scratch_shapes=[
            pltpu.VMEM((8, 16, 4096 + 128), BF),
            pltpu.VMEM((1, 4096), BF),
            pltpu.VMEM((1, 128), jnp.int32),
            pltpu.VMEM((1, 128), jnp.int32),
            pltpu.SemaphoreType.DMA((4,)),
        ],
        **tiny(40),
    )(got, head_weight.reshape(1, 4096), prompt_ids.reshape(1, 128), cluster_ids.reshape(1, 128))


def vote_kernel(all_hbm, scores_ref, votes_ref, x3, x, vals, ids, votes, sem):
    copy = pltpu.make_async_copy(all_hbm, x3, sem)
    copy.start()
    copy.wait()
    x[...] = x3[...].reshape(128, 128)
    t = lax.axis_index(TP)
    lane8 = lax.broadcasted_iota(jnp.int32, (8, 128), 1)
    row8 = lax.broadcasted_iota(jnp.int32, (8, 128), 0)
    lane = lax.broadcasted_iota(jnp.int32, (16, 128), 1)
    place = lane8 // 16 == row8

    def line(block, first):
        front = pltpu.roll(block, 128 - first, 1) if first else block
        rolled = pltpu.roll(front, 0, 1, stride=16, stride_axis=0)
        return jnp.sum(jnp.where(place, rolled, 0.0), axis=0, keepdims=True)

    def scores_of(zx, c):
        base = (zx & 1) * 64 + c * 8 + (zx >> 1) * 2
        return jnp.concatenate(
            [x[pl.ds(base, 4, stride=16), :], x[pl.ds(base + 1, 4, stride=16), :]], axis=0
        )

    for c in range(2):
        scores_ref[c : c + 1, :] = line(scores_of(t, c), 0)
    for zx in range(8):
        for c in range(2):
            dp = zx * 2 + c
            vals[dp : dp + 1, :] = line(scores_of(zx, c), 0)
            ids[dp : dp + 1, :] = line(x[dp * 8 : dp * 8 + 8, :], 16)
    votes[...] = jnp.zeros((128, 128), F32)
    for p in range(2):
        acc = jnp.zeros((16, 128), F32)
        for k in range(CLUSTERS):
            hit = jnp.where(ids[...] == float(p * CLUSTERS + k), vals[...], 0.0)
            acc = jnp.where(lane == k, jnp.sum(hit, axis=1, keepdims=True), acc)
        votes[pl.ds(p, 16, stride=2), :] = acc
    votes_ref[...] = votes[...].T[:CLUSTERS, :32]


def tally(everyone):
    V = pl.BlockSpec(memory_space=pltpu.VMEM)
    A = pl.BlockSpec(memory_space=pl.ANY)
    return pl.pallas_call(
        vote_kernel,
        out_shape=(jax.ShapeDtypeStruct((2, 128), F32), jax.ShapeDtypeStruct((CLUSTERS, 32), F32)),
        in_specs=[A],
        out_specs=(V, V),
        scratch_shapes=[
            pltpu.VMEM((128, 1, 128), F32),
            pltpu.VMEM((128, 128), F32),
            pltpu.VMEM((16, 128), F32),
            pltpu.VMEM((16, 128), F32),
            pltpu.VMEM((128, 128), F32),
            pltpu.SemaphoreType.DMA,
        ],
        **tiny(40),
    )(everyone)


def body(
    queries,
    new_key,
    new_value,
    cache_keys,
    cache_values,
    lengths,
    prefix_keys,
    prefix_values,
    prompt_ids,
    cluster_ids,
    out_weight,
    residual,
    norm_gain,
    up_weight,
    head_weight,
):
    c = lax.axis_index("c")
    yl = lax.axis_index("yl")

    def rows_of(x, first, count):
        return lax.dynamic_slice_in_dim(x, first, count, 0)

    w10 = swap(out_weight, "xh")
    up_par = swap(up_weight, "c")
    w01 = swap(out_weight, "c")

    part = attend(
        queries,
        new_key,
        new_value,
        cache_keys,
        cache_values,
        lengths,
        prefix_keys,
        prefix_values,
        prompt_ids,
    )

    part = hold(part, up_par, w01, mib=63)
    before, after = shift(part, 1), shift(part, 3)
    far = (shift(before[:64], 1), shift(after[64:], 3))
    gain = jnp.broadcast_to(norm_gain[None, :], (16, 512))
    gain_par = swap(gain, "c")
    later = hold(residual, part)
    extra = swap(rows_of(later, (1 - c) * 128, 128), "c")
    res_y = swap(
        jnp.concatenate(
            [rows_of(later, c * 128 + (1 - yl) * 64, 64), rows_of(extra, (1 - yl) * 64, 64)], axis=1
        ),
        "yl",
    )
    w10 = hold(w10, before, after, res_y)
    w11 = swap(w10, "c")

    weights = (out_weight, w01, w10, w11)
    partial = project((0, 1, 3), part, before, after, *weights)
    partial = project((2,), *far, *weights, partial)
    parts = lax.all_to_all(partial, ("xh", "xl", "yh", "yl"), 0, 0, tiled=True)
    hid_mine, hid_par, sent = verify_up(parts, residual, extra, res_y, gain, gain_par, up_weight, up_par)
    got = lax.all_to_all(sent.reshape(8, 16, 4096 + 128), ("z", "xh"), 0, 0, tiled=True)

    hid_back = swap(hid_par, "c")
    away = jnp.concatenate([rows_of(hid_mine, (1 - yl) * 64, 64), rows_of(hid_back, (1 - yl) * 64, 64)], axis=1)
    home = jnp.concatenate([rows_of(hid_mine, yl * 64, 64), rows_of(hid_back, yl * 64, 64)], axis=1)
    came = swap(away, "yl")
    block = jnp.where(
        yl == 0, jnp.concatenate([home, came], axis=0), jnp.concatenate([came, home], axis=0)
    )
    mine, back = block[:, :512], block[:, 512:]
    hidden = jnp.where(
        c == 0, jnp.concatenate([mine, back], axis=0), jnp.concatenate([back, mine], axis=0)
    )

    line = score(got, head_weight, prompt_ids, cluster_ids)
    scores, votes = tally(lax.all_to_all(line, AXES, 0, 0, tiled=True))
    return hidden, scores.reshape(256), votes.T


def solution(mesh):
    fine = Mesh(mesh.devices.reshape(4, 2, 2, 2, 2, 2), AXES)
    placed = (
        P(DP, TP),
        P(DP, TP),
        P(DP, TP),
        P(DP, TP, None, None),
        P(DP, TP, None, None),
        P(DP),
        P(DP, TP, None, None),
        P(DP, TP, None, None),
        P(DP),
        P(DP),
        P(TP, DP),
        P(TP, DP),
        P(DP),
        P(DP, None),
        P(),
    )
    return jax.shard_map(
        body,
        mesh=fine,
        in_specs=placed,
        out_specs=(P(TP, DP), P(TP), P()),
        check_vma=False,
    )
```

```python
import functools
import math

import jax
import jax.numpy as jnp
from jax import lax
from jax.experimental import pallas as pl
from jax.experimental.pallas import tpu as pltpu
from jax.sharding import Mesh, PartitionSpec as P

D = 8192
CLUSTERS = 16
PROMPTS_DEV = 2
eps = 1e-05
AXES = ("z", "xh", "c", "xl", "yh", "yl")
DP = ("z", "xh", "c")
TP = ("xl", "yh", "yl")
BF = jnp.bfloat16
F32 = jnp.float32
SCALE2 = math.log2(math.e) / math.sqrt(128)
NEG = -1e30
LIMIT = 63 * 1024 * 1024
NT = (((1,), (1,)), ((), ()))


def attn_kernel(rows, tile, ids_hbm, ids2_hbm, lens_hbm, q_hbm, nk_hbm, nv_hbm, pk_hbm, pv_hbm, ck_hbm, cv_hbm,
                out_ref, ids_s, ids_v, lens_v, q_ref, nk_ref, nv_ref, pk, pv, ck, cv, qs, nks, nvs, lens, acc,
                mbuf, lbuf, s_scr, sem_i, sem_p, sem_k, sem_v):
    small = [pltpu.make_async_copy(h, v, sem_i.at[i]) for i, (h, v) in enumerate((
        (ids_hbm, ids_s), (ids2_hbm, ids_v), (lens_hbm, lens_v), (q_hbm, q_ref), (nk_hbm, nk_ref), (nv_hbm, nv_ref)))]
    for cp in small:
        cp.start()
    heads = q_ref.shape[1] // 128
    tiles = rows // tile
    ctile = 16
    ctiles = rows // ctile
    keys = pk.shape[1]
    pre = [pltpu.make_async_copy(h.at[p], v.at[p], sem_p.at[p, i])
           for p in range(2) for i, (h, v) in enumerate(((pk_hbm, pk), (pv_hbm, pv)))]
    for cp in pre:
        cp.start()

    small[0].wait()

    def place(r, counts):
        c0, c1 = counts
        p = ids_s[r] & 1
        to = jnp.where(p == 0, c0, rows - 1 - c1)
        blk = to // ctile
        pltpu.make_async_copy(ck_hbm.at[r], ck.at[to], sem_k.at[blk]).start()
        pltpu.make_async_copy(cv_hbm.at[r], cv.at[to], sem_v.at[blk]).start()
        return c0 + 1 - p, c1 + p

    n0, _ = lax.fori_loop(0, rows, place, (jnp.int32(0), jnp.int32(0)), unroll=8)

    for cp in small[1:]:
        cp.wait()
    second = (ids_v[...] & 1)
    ones = jnp.broadcast_to(second, (rows, rows)).astype(F32).astype(BF)
    ri = lax.broadcasted_iota(jnp.int32, (rows, rows), 0)
    ci = lax.broadcasted_iota(jnp.int32, (rows, rows), 1)
    upper = (ri < ci).astype(F32).astype(BF)
    before1 = jnp.dot(ones, upper, preferred_element_type=F32)
    pos = jnp.where(jnp.broadcast_to(second, (rows, rows)) == 0, ci.astype(F32) - before1, rows - 1 - before1)
    perm32 = (pos == ri.astype(F32)).astype(F32)
    perm = perm32.astype(BF)
    unperm = perm32.T.astype(BF)
    qs[...] = jnp.dot(perm, q_ref[...], preferred_element_type=F32).astype(BF)
    nks[...] = jnp.dot(perm, nk_ref[...], preferred_element_type=F32)
    nvs[...] = jnp.dot(perm, nv_ref[...], preferred_element_type=F32)
    lb = jnp.broadcast_to(lens_v[...], (128, rows)).astype(F32).astype(BF)
    lens[...] = lax.dot_general(perm, lb, NT, preferred_element_type=F32)

    for cp in pre:
        cp.wait()
    edge = jnp.minimum(n0 // tile, tiles - 1)
    chunk = 512

    def prefix(item, _):
        p = (item > edge).astype(jnp.int32)
        row0 = pl.multiple_of((item - p) * tile, tile)
        qt = jnp.concatenate([qs[pl.ds(row0, tile), h * 128:(h + 1) * 128] for h in range(heads)], axis=0)
        top = None
        for k in range(0, keys, chunk):
            s = lax.dot_general(qt, pk[p, k:k + chunk], NT, preferred_element_type=F32)
            s_scr[:, k:k + chunk] = s
            for j in range(0, chunk, 128):
                top = s[:, j:j + 128] if top is None else jnp.maximum(top, s[:, j:j + 128])
        m = jnp.max(top, axis=1, keepdims=True)
        mb = jnp.broadcast_to(m, (heads * tile, 128))
        l = jnp.zeros((heads * tile, 128), F32)
        o = jnp.zeros((heads * tile, 128), F32)
        for k in range(0, keys, chunk):
            ps = []
            for j in range(0, chunk, 128):
                e = jnp.exp2((s_scr[:, k + j:k + j + 128] - mb) * SCALE2)
                l = l + e
                ps.append(e.astype(BF))
            o = o + jnp.dot(jnp.concatenate(ps, axis=1), pv[p, k:k + chunk], preferred_element_type=F32)
        lsum = jnp.broadcast_to(jnp.sum(l, axis=1, keepdims=True), (heads * tile, 128))
        at = row0 + lax.broadcasted_iota(jnp.int32, (tile, 128), 0)
        mine = (at < n0) == (p == 0)
        for h in range(heads):
            hs = slice(h * tile, (h + 1) * tile)
            cs = slice(h * 128, (h + 1) * 128)
            rs = pl.ds(row0, tile)
            acc[rs, cs] = jnp.where(mine, o[hs], acc[rs, cs])
            mbuf[rs, cs] = jnp.where(mine, mb[hs], mbuf[rs, cs])
            lbuf[rs, cs] = jnp.where(mine, lsum[hs], lbuf[rs, cs])
        return 0

    lax.fori_loop(0, tiles + 1, prefix, 0)

    mrow = lax.broadcasted_iota(jnp.int32, (heads * ctile, 128), 0) % ctile
    lane = lax.broadcasted_iota(jnp.int32, (heads * ctile, 128), 1).astype(F32)

    def cached(b, _):
        r0 = pl.multiple_of(b * ctile, ctile)
        rs = pl.ds(r0, ctile)
        pltpu.make_async_copy(ck_hbm.at[pl.ds(0, ctile)], ck.at[rs], sem_k.at[b]).wait()
        pltpu.make_async_copy(cv_hbm.at[pl.ds(0, ctile)], cv.at[rs], sem_v.at[b]).wait()
        heads_of = lambda ref: jnp.concatenate([ref[rs, h * 128:(h + 1) * 128] for h in range(heads)], axis=0)
        rep = lambda x: jnp.concatenate([x] * heads, axis=0)
        qt = heads_of(qs)
        kt = ck[rs].reshape(ctile * 128, 128)
        vt = cv[rs].reshape(ctile * 128, 128)
        s = lax.dot_general(qt, kt, NT, preferred_element_type=F32)
        sc = s[:, :128]
        for r in range(1, ctile):
            sc = jnp.where(mrow == r, s[:, r * 128:(r + 1) * 128], sc)
        sc = jnp.where(lane < rep(lens[rs]), sc, NEG)
        so = jnp.sum(qt.astype(F32) * rep(nks[rs]), axis=1, keepdims=True)
        mp = heads_of(mbuf)
        m = jnp.maximum(jnp.maximum(mp, jnp.max(sc, axis=1, keepdims=True)), so)
        ap = jnp.exp2((mp - m) * SCALE2)
        e = jnp.exp2((sc - m) * SCALE2)
        eo = jnp.exp2((so - m) * SCALE2)
        eb = e.astype(BF).astype(F32)
        pe = jnp.concatenate([jnp.where(mrow == r, eb, 0.0).astype(BF) for r in range(ctile)], axis=1)
        oc = jnp.dot(pe, vt, preferred_element_type=F32)
        l = ap * heads_of(lbuf) + jnp.sum(e, axis=1, keepdims=True) + eo
        o = (ap * heads_of(acc) + oc + eo * rep(nvs[rs])) / l
        for h in range(heads):
            qs[rs, h * 128:(h + 1) * 128] = o[h * ctile:(h + 1) * ctile].astype(BF)
        return 0

    lax.fori_loop(0, ctiles, cached, 0)
    out_ref[...] = jnp.dot(unperm, qs[...], preferred_element_type=F32).astype(BF)


def attend(queries, new_key, new_value, ck, cv, lengths, pk, pv, prompt_ids, tile=32):
    rows = queries.shape[0]
    width = queries.shape[1]
    keys = pk.shape[2]
    heads = width // 128
    V = pl.BlockSpec(memory_space=pltpu.VMEM)
    A = pl.BlockSpec(memory_space=pl.ANY)
    S = pl.BlockSpec(memory_space=pltpu.SMEM)
    return pl.pallas_call(
        functools.partial(attn_kernel, rows, tile),
        out_shape=jax.ShapeDtypeStruct((rows, width), BF),
        in_specs=[A] * 10,
        out_specs=V,
        scratch_shapes=[
            pltpu.SMEM((rows,), jnp.int32), pltpu.VMEM((1, rows), jnp.int32), pltpu.VMEM((1, rows), jnp.int32),
            pltpu.VMEM((rows, width), BF), pltpu.VMEM((rows, 128), BF), pltpu.VMEM((rows, 128), BF),
            pltpu.VMEM((2, keys, 128), BF), pltpu.VMEM((2, keys, 128), BF),
            pltpu.VMEM((rows, 128, 128), BF), pltpu.VMEM((rows, 128, 128), BF),
            pltpu.VMEM((rows, width), BF), pltpu.VMEM((rows, 128), F32), pltpu.VMEM((rows, 128), F32),
            pltpu.VMEM((rows, 128), F32),
            pltpu.VMEM((rows, width), F32), pltpu.VMEM((rows, width), F32), pltpu.VMEM((rows, width), F32),
            pltpu.VMEM((heads * tile, keys), F32),
            pltpu.SemaphoreType.DMA((6,)), pltpu.SemaphoreType.DMA((2, 2)), pltpu.SemaphoreType.DMA((rows // 16,)), pltpu.SemaphoreType.DMA((rows // 16,)),
        ],
        compiler_params=pltpu.CompilerParams(vmem_limit_bytes=LIMIT),
        cost_estimate=pl.CostEstimate(flops=16 * 10**9, bytes_accessed=11 * 1024 * 1024, transcendentals=2 * 1024 * 1024),
    )(prompt_ids, prompt_ids.reshape(1, rows), lengths.reshape(1, rows), queries, new_key, new_value,
      pk.reshape(2, keys, 128), pv.reshape(2, keys, 128), ck.reshape(rows, 128, 128), cv.reshape(rows, 128, 128))


def swap(x, axis):
    return lax.ppermute(x, axis, [(0, 1), (1, 0)])


def shift(x, by):
    return lax.ppermute(x, "z", [(i, (i + by) % 4) for i in range(4)])


def tiny(mib, flops=1024, **kw):
    return dict(
        compiler_params=pltpu.CompilerParams(vmem_limit_bytes=mib * 1024 * 1024),
        cost_estimate=pl.CostEstimate(flops=flops, bytes_accessed=1024, transcendentals=0),
        **kw,
    )


def hold_kernel(*refs):
    pass


def hold(x, *tokens, mib=4):
    A = pl.BlockSpec(memory_space=pl.ANY)
    return pl.pallas_call(
        hold_kernel,
        out_shape=jax.ShapeDtypeStruct(x.shape, x.dtype),
        in_specs=[A] * (1 + len(tokens)),
        out_specs=A,
        input_output_aliases={0: 0},
        **tiny(mib),
    )(x, *tokens)


def proj_kernel(steps, *refs):
    count = len(steps)
    given = len(refs) - 8 - (count == 1)
    rows, weights = refs[:given], refs[given : given + 4]
    out, w, chunks, sems = refs[-4:]
    loads = [
        pltpu.make_async_copy(src, w.at[:, j * 512 : (j + 1) * 512], sems.at[j])
        for j, src in enumerate(weights)
    ]
    for load in loads:
        load.start()
    a = jnp.concatenate([row[...] for row in rows], axis=0)
    z = lax.axis_index("z")
    xh = lax.axis_index("xh")
    leave = []
    for j in range(4):
        loads[j].wait()
        total = jnp.dot(a, w[:, j * 512 : (j + 1) * 512], preferred_element_type=F32).astype(BF)
        total = total.reshape(count, 2, 64, 512)
        for i in range(count):
            chunks[j // 2, i, :, :, (j % 2) * 512 : (j % 2 + 1) * 512] = total[i]
        if j % 2:
            for i, step in enumerate(steps):
                first = ((xh ^ (j // 2)) * 4 + ((z - step) & 3)) * 2
                leave.append(
                    pltpu.make_async_copy(chunks.at[j // 2, i], out.at[pl.ds(first, 2)], sems.at[4 + j // 2 * count + i])
                )
                leave[-1].start()
    for copy in leave:
        copy.wait()


def project(steps, *ins):
    count = len(steps)
    more = count == 1
    given = len(ins) - 4 - more
    V = pl.BlockSpec(memory_space=pltpu.VMEM)
    A = pl.BlockSpec(memory_space=pl.ANY)
    return pl.pallas_call(
        functools.partial(proj_kernel, steps),
        out_shape=jax.ShapeDtypeStruct((16, 64, 1024), BF),
        in_specs=[V] * given + [A] * (len(ins) - given),
        out_specs=A,
        input_output_aliases={given + 4: 0} if more else {},
        scratch_shapes=[
            pltpu.VMEM((1024, 2048), BF),
            pltpu.VMEM((2, count, 2, 64, 1024), BF),
            pltpu.SemaphoreType.DMA((4 + 2 * count,)),
        ],
        **tiny(48, 0),
    )(*ins)


def up_kernel(
    parts, res, extra, res_y, gain, gain_par, up_mine, up_par,
    hm_ref, hp_ref, sent_ref, res_v, gain_v, gain2_v, w, sent, sems,
):
    c = lax.axis_index("c")
    yl = lax.axis_index("yl")
    here = pl.ds(pl.multiple_of(yl * 64, 64), 64)
    there = pl.ds(pl.multiple_of(64 - yl * 64, 64), 64)
    small = [
        pltpu.make_async_copy(src, dst, sems.at[i // 4, i % 4])
        for i, (src, dst) in enumerate((
            (res.at[pl.ds(pl.multiple_of(c * 128 + yl * 64, 64), 64)], res_v.at[here, :512]),
            (extra.at[here], res_v.at[here, 512:]),
            (res_y, res_v.at[there]),
            (gain, gain_v), (gain_par, gain2_v),
        ))
    ]
    loads = []
    for j in range(4):
        cols = slice(j * 1024, (j + 1) * 1024)
        loads.append((
            pltpu.make_async_copy(up_mine.at[:, cols], w.at[0:512, cols], sems.at[2, j]),
            pltpu.make_async_copy(up_par.at[:, cols], w.at[512:1024, cols], sems.at[3, j]),
        ))
        for load in loads[-1]:
            load.start()
        if j == 0:
            for copy in small:
                copy.start()
    for copy in small:
        copy.wait()

    def summed(first):
        total = parts[first].astype(F32)
        for i in range(1, 8):
            total = total + parts[first + i].astype(F32)
        return total

    mixed = jnp.concatenate([summed(0), summed(8)], axis=0)
    hid = (res_v[...].astype(F32) + mixed).astype(BF)
    hm_ref[...] = hid[:, :512]
    hp_ref[...] = hid[:, 512:]
    wide = hid.astype(F32)
    squares = jnp.sum(wide * wide, axis=1, keepdims=True)
    hi = squares.astype(BF).astype(F32)
    lane = lax.broadcasted_iota(jnp.int32, (128, 128), 1)
    sent[:, 4096:] = jnp.where(lane == 0, hi, jnp.where(lane == 1, squares - hi, 0.0)).astype(BF)
    gains = jnp.concatenate([gain_v[0:1], gain2_v[0:1]], axis=1).astype(F32)
    gained = (wide * gains).astype(BF)
    leave = []
    for j in range(4):
        cols = slice(j * 1024, (j + 1) * 1024)
        for load in loads[j]:
            load.wait()
        sent[:, cols] = jnp.dot(gained, w[:, cols], preferred_element_type=F32).astype(BF)
        out = slice(j * 1024, (j + 1) * 1024 + (128 if j == 3 else 0))
        leave.append(pltpu.make_async_copy(sent.at[:, out], sent_ref.at[:, out], sems.at[4, j]))
        leave[-1].start()
    for copy in leave:
        copy.wait()


def verify_up(*ins):
    V = pl.BlockSpec(memory_space=pltpu.VMEM)
    A = pl.BlockSpec(memory_space=pl.ANY)
    return pl.pallas_call(
        up_kernel,
        out_shape=(
            jax.ShapeDtypeStruct((128, 512), BF),
            jax.ShapeDtypeStruct((128, 512), BF),
            jax.ShapeDtypeStruct((128, 4096 + 128), BF),
        ),
        in_specs=[V] + [A] * 7,
        out_specs=(V, V, A),
        scratch_shapes=[
            pltpu.VMEM((128, 1024), BF),
            pltpu.VMEM((16, 512), BF),
            pltpu.VMEM((16, 512), BF),
            pltpu.VMEM((1024, 4096), BF),
            pltpu.VMEM((128, 4096 + 128), BF),
            pltpu.SemaphoreType.DMA((5, 4)),
        ],
        **tiny(48),
    )(*ins)


def score_kernel(got_hbm, head_hbm, prompts_hbm, clusters_hbm, out_ref, got, head, prompts, clusters, sems):
    copies = [
        pltpu.make_async_copy(src, dst, sems.at[i])
        for i, (src, dst) in enumerate((
            (got_hbm, got), (head_hbm, head), (prompts_hbm, prompts), (clusters_hbm, clusters)
        ))
    ]
    for copy in copies:
        copy.start()
    for copy in copies:
        copy.wait()

    def summed(cols):
        total = got[0, :, cols].astype(F32)
        for i in range(1, 8):
            total = total + got[i, :, cols].astype(F32)
        return total

    tail = summed(slice(4096, 4224))
    squares = tail[:, 0:1] + tail[:, 1:2]
    factor = lax.rsqrt(squares / D + eps)
    acc = jnp.zeros((16, 512), F32)
    for j in range(0, 4096, 512):
        cols = slice(j, j + 512)
        up = summed(cols) * factor
        acc = acc + up / (1.0 + jnp.exp(-up)) * head[0:1, cols].astype(F32)
    scores = jnp.sum(acc, axis=1, keepdims=True)
    row = lax.broadcasted_iota(jnp.int32, (16, 128), 0)
    lane = lax.broadcasted_iota(jnp.int32, (16, 128), 1)
    line = jnp.sum(jnp.where(row == lane, scores, 0.0), axis=0, keepdims=True)
    pair = ((prompts[...] & 1) * CLUSTERS + clusters[...]).astype(F32)
    t = lax.axis_index(TP)
    pair = pltpu.roll(jnp.broadcast_to(pair, (8, 128)), (144 - t * 16) & 127, 1)[0:1]
    lane = lane[0:1]
    mine = jnp.where(lane < 16, line, jnp.where(lane < 32, pair, 0.0))
    out_ref[...] = jnp.broadcast_to(mine.reshape(1, 1, 128), (128, 1, 128))


def score(got, head_weight, prompt_ids, cluster_ids):
    V = pl.BlockSpec(memory_space=pltpu.VMEM)
    A = pl.BlockSpec(memory_space=pl.ANY)
    return pl.pallas_call(
        score_kernel,
        out_shape=jax.ShapeDtypeStruct((128, 1, 128), F32),
        in_specs=[A] * 4,
        out_specs=V,
        scratch_shapes=[
            pltpu.VMEM((8, 16, 4096 + 128), BF),
            pltpu.VMEM((1, 4096), BF),
            pltpu.VMEM((1, 128), jnp.int32),
            pltpu.VMEM((1, 128), jnp.int32),
            pltpu.SemaphoreType.DMA((4,)),
        ],
        **tiny(40),
    )(got, head_weight.reshape(1, 4096), prompt_ids.reshape(1, 128), cluster_ids.reshape(1, 128))


def vote_kernel(all_hbm, scores_ref, votes_ref, x3, x, vals, ids, votes, sem):
    copy = pltpu.make_async_copy(all_hbm, x3, sem)
    copy.start()
    copy.wait()
    x[...] = x3[...].reshape(128, 128)
    t = lax.axis_index(TP)
    lane8 = lax.broadcasted_iota(jnp.int32, (8, 128), 1)
    row8 = lax.broadcasted_iota(jnp.int32, (8, 128), 0)
    lane = lax.broadcasted_iota(jnp.int32, (16, 128), 1)
    place = lane8 // 16 == row8

    def line(block, first):
        front = pltpu.roll(block, 128 - first, 1) if first else block
        rolled = pltpu.roll(front, 0, 1, stride=16, stride_axis=0)
        return jnp.sum(jnp.where(place, rolled, 0.0), axis=0, keepdims=True)

    def scores_of(zx, c):
        base = (zx & 1) * 64 + c * 8 + (zx >> 1) * 2
        return jnp.concatenate(
            [x[pl.ds(base, 4, stride=16), :], x[pl.ds(base + 1, 4, stride=16), :]], axis=0
        )

    for c in range(2):
        scores_ref[c : c + 1, :] = line(scores_of(t, c), 0)
    for zx in range(8):
        for c in range(2):
            dp = zx * 2 + c
            vals[dp : dp + 1, :] = line(scores_of(zx, c), 0)
            ids[dp : dp + 1, :] = line(x[dp * 8 : dp * 8 + 8, :], 16)
    votes[...] = jnp.zeros((128, 128), F32)
    for p in range(2):
        acc = jnp.zeros((16, 128), F32)
        for k in range(CLUSTERS):
            hit = jnp.where(ids[...] == float(p * CLUSTERS + k), vals[...], 0.0)
            acc = jnp.where(lane == k, jnp.sum(hit, axis=1, keepdims=True), acc)
        votes[pl.ds(p, 16, stride=2), :] = acc
    votes_ref[...] = votes[...].T[:CLUSTERS, :32]


def tally(everyone):
    V = pl.BlockSpec(memory_space=pltpu.VMEM)
    A = pl.BlockSpec(memory_space=pl.ANY)
    return pl.pallas_call(
        vote_kernel,
        out_shape=(jax.ShapeDtypeStruct((2, 128), F32), jax.ShapeDtypeStruct((CLUSTERS, 32), F32)),
        in_specs=[A],
        out_specs=(V, V),
        scratch_shapes=[
            pltpu.VMEM((128, 1, 128), F32),
            pltpu.VMEM((128, 128), F32),
            pltpu.VMEM((16, 128), F32),
            pltpu.VMEM((16, 128), F32),
            pltpu.VMEM((128, 128), F32),
            pltpu.SemaphoreType.DMA,
        ],
        **tiny(40),
    )(everyone)


def body(
    queries,
    new_key,
    new_value,
    cache_keys,
    cache_values,
    lengths,
    prefix_keys,
    prefix_values,
    prompt_ids,
    cluster_ids,
    out_weight,
    residual,
    norm_gain,
    up_weight,
    head_weight,
):
    c = lax.axis_index("c")
    yl = lax.axis_index("yl")

    def rows_of(x, first, count):
        return lax.dynamic_slice_in_dim(x, first, count, 0)

    w10 = swap(out_weight, "xh")
    up_par = swap(up_weight, "c")
    w01 = swap(out_weight, "c")

    part = attend(
        queries,
        new_key,
        new_value,
        cache_keys,
        cache_values,
        lengths,
        prefix_keys,
        prefix_values,
        prompt_ids,
    )

    part = hold(part, up_par, w01, mib=63)
    before, after = shift(part, 1), shift(part, 3)
    far = (shift(before[:64], 1), shift(after[64:], 3))
    later = hold(residual, part)
    gain = norm_gain[None, :] + later[:16] * 0
    gain_par = swap(gain, "c")
    extra = swap(rows_of(later, (1 - c) * 128, 128), "c")
    res_y = swap(
        jnp.concatenate(
            [rows_of(later, c * 128 + (1 - yl) * 64, 64), rows_of(extra, (1 - yl) * 64, 64)], axis=1
        ),
        "yl",
    )
    w10 = hold(w10, before, after, res_y, gain_par)
    w11 = swap(w10, "c")

    weights = (out_weight, w01, w10, w11)
    partial = project((0, 1, 3), part, before, after, *weights)
    partial = project((2,), *far, *weights, partial)
    parts = lax.all_to_all(partial, ("xh", "xl", "yh", "yl"), 0, 0, tiled=True)
    hid_mine, hid_par, sent = verify_up(parts, residual, extra, res_y, gain, gain_par, up_weight, up_par)
    got = lax.all_to_all(sent.reshape(8, 16, 4096 + 128), ("z", "xh"), 0, 0, tiled=True)

    hid_back = swap(hid_par, "c")
    away = jnp.concatenate([rows_of(hid_mine, (1 - yl) * 64, 64), rows_of(hid_back, (1 - yl) * 64, 64)], axis=1)
    home = jnp.concatenate([rows_of(hid_mine, yl * 64, 64), rows_of(hid_back, yl * 64, 64)], axis=1)
    came = swap(away, "yl")
    block = jnp.where(
        yl == 0, jnp.concatenate([home, came], axis=0), jnp.concatenate([came, home], axis=0)
    )
    mine, back = block[:, :512], block[:, 512:]
    hidden = jnp.where(
        c == 0, jnp.concatenate([mine, back], axis=0), jnp.concatenate([back, mine], axis=0)
    )

    line = score(got, head_weight, prompt_ids, cluster_ids)
    scores, votes = tally(lax.all_to_all(line, AXES, 0, 0, tiled=True))
    return hidden, scores.reshape(256), votes.T


def solution(mesh):
    fine = Mesh(mesh.devices.reshape(4, 2, 2, 2, 2, 2), AXES)
    placed = (
        P(DP, TP),
        P(DP, TP),
        P(DP, TP),
        P(DP, TP, None, None),
        P(DP, TP, None, None),
        P(DP),
        P(DP, TP, None, None),
        P(DP, TP, None, None),
        P(DP),
        P(DP),
        P(TP, DP),
        P(TP, DP),
        P(DP),
        P(DP, None),
        P(),
    )
    return jax.shard_map(
        body,
        mesh=fine,
        in_specs=placed,
        out_specs=(P(TP, DP), P(TP), P()),
        check_vma=False,
    )
```

```python
import functools
import math

import jax
import jax.numpy as jnp
from jax import lax
from jax.experimental import pallas as pl
from jax.experimental.pallas import tpu as pltpu
from jax.sharding import Mesh, PartitionSpec as P

D = 8192
CLUSTERS = 16
PROMPTS_DEV = 2
eps = 1e-05
AXES = ("z", "xh", "c", "xl", "yh", "yl")
DP = ("z", "xh", "c")
TP = ("xl", "yh", "yl")
BF = jnp.bfloat16
F32 = jnp.float32
SCALE2 = math.log2(math.e) / math.sqrt(128)
NEG = -1e30
LIMIT = 63 * 1024 * 1024
NT = (((1,), (1,)), ((), ()))


def attn_kernel(rows, tile, ids_hbm, ids2_hbm, lens_hbm, q_hbm, nk_hbm, nv_hbm, pk_hbm, pv_hbm, ck_hbm, cv_hbm,
                out_ref, ids_s, ids_v, lens_v, q_ref, nk_ref, nv_ref, pk, pv, ck, cv, qs, nks, nvs, lens, acc,
                mbuf, lbuf, s_scr, sem_i, sem_p, sem_k, sem_v):
    small = [pltpu.make_async_copy(h, v, sem_i.at[i]) for i, (h, v) in enumerate((
        (ids_hbm, ids_s), (ids2_hbm, ids_v), (lens_hbm, lens_v), (q_hbm, q_ref), (nk_hbm, nk_ref), (nv_hbm, nv_ref)))]
    for cp in small:
        cp.start()
    heads = q_ref.shape[1] // 128
    tiles = rows // tile
    ctile = 16
    ctiles = rows // ctile
    keys = pk.shape[1]
    pre = [pltpu.make_async_copy(h.at[p], v.at[p], sem_p.at[p, i])
           for p in range(2) for i, (h, v) in enumerate(((pk_hbm, pk), (pv_hbm, pv)))]
    for cp in pre:
        cp.start()

    small[0].wait()

    def place(r, counts):
        c0, c1 = counts
        p = ids_s[r] & 1
        to = jnp.where(p == 0, c0, rows - 1 - c1)
        blk = to // ctile
        pltpu.make_async_copy(ck_hbm.at[r], ck.at[to], sem_k.at[blk]).start()
        pltpu.make_async_copy(cv_hbm.at[r], cv.at[to], sem_v.at[blk]).start()
        return c0 + 1 - p, c1 + p

    n0, _ = lax.fori_loop(0, rows, place, (jnp.int32(0), jnp.int32(0)), unroll=8)

    for cp in small[1:]:
        cp.wait()
    second = (ids_v[...] & 1)
    ones = jnp.broadcast_to(second, (rows, rows)).astype(F32).astype(BF)
    ri = lax.broadcasted_iota(jnp.int32, (rows, rows), 0)
    ci = lax.broadcasted_iota(jnp.int32, (rows, rows), 1)
    upper = (ri < ci).astype(F32).astype(BF)
    before1 = jnp.dot(ones, upper, preferred_element_type=F32)
    pos = jnp.where(jnp.broadcast_to(second, (rows, rows)) == 0, ci.astype(F32) - before1, rows - 1 - before1)
    perm32 = (pos == ri.astype(F32)).astype(F32)
    perm = perm32.astype(BF)
    unperm = perm32.T.astype(BF)
    qs[...] = jnp.dot(perm, q_ref[...], preferred_element_type=F32).astype(BF)
    nks[...] = jnp.dot(perm, nk_ref[...], preferred_element_type=F32)
    nvs[...] = jnp.dot(perm, nv_ref[...], preferred_element_type=F32)
    lb = jnp.broadcast_to(lens_v[...], (128, rows)).astype(F32).astype(BF)
    lens[...] = lax.dot_general(perm, lb, NT, preferred_element_type=F32)

    for cp in pre:
        cp.wait()
    edge = jnp.minimum(n0 // tile, tiles - 1)
    chunk = 512

    def prefix(item, _):
        p = (item > edge).astype(jnp.int32)
        row0 = pl.multiple_of((item - p) * tile, tile)
        qt = jnp.concatenate([qs[pl.ds(row0, tile), h * 128:(h + 1) * 128] for h in range(heads)], axis=0)
        top = None
        for k in range(0, keys, chunk):
            s = lax.dot_general(qt, pk[p, k:k + chunk], NT, preferred_element_type=F32)
            s_scr[:, k:k + chunk] = s
            for j in range(0, chunk, 128):
                top = s[:, j:j + 128] if top is None else jnp.maximum(top, s[:, j:j + 128])
        m = jnp.max(top, axis=1, keepdims=True)
        mb = jnp.broadcast_to(m, (heads * tile, 128))
        l = jnp.zeros((heads * tile, 128), F32)
        o = jnp.zeros((heads * tile, 128), F32)
        for k in range(0, keys, chunk):
            ps = []
            for j in range(0, chunk, 128):
                e = jnp.exp2((s_scr[:, k + j:k + j + 128] - mb) * SCALE2)
                l = l + e
                ps.append(e.astype(BF))
            o = o + jnp.dot(jnp.concatenate(ps, axis=1), pv[p, k:k + chunk], preferred_element_type=F32)
        lsum = jnp.broadcast_to(jnp.sum(l, axis=1, keepdims=True), (heads * tile, 128))
        at = row0 + lax.broadcasted_iota(jnp.int32, (tile, 128), 0)
        mine = (at < n0) == (p == 0)
        for h in range(heads):
            hs = slice(h * tile, (h + 1) * tile)
            cs = slice(h * 128, (h + 1) * 128)
            rs = pl.ds(row0, tile)
            acc[rs, cs] = jnp.where(mine, o[hs], acc[rs, cs])
            mbuf[rs, cs] = jnp.where(mine, mb[hs], mbuf[rs, cs])
            lbuf[rs, cs] = jnp.where(mine, lsum[hs], lbuf[rs, cs])
        return 0

    lax.fori_loop(0, tiles + 1, prefix, 0)

    mrow = lax.broadcasted_iota(jnp.int32, (heads * ctile, 128), 0) % ctile
    lane = lax.broadcasted_iota(jnp.int32, (heads * ctile, 128), 1).astype(F32)

    def cached(b, _):
        r0 = pl.multiple_of(b * ctile, ctile)
        rs = pl.ds(r0, ctile)
        pltpu.make_async_copy(ck_hbm.at[pl.ds(0, ctile)], ck.at[rs], sem_k.at[b]).wait()
        pltpu.make_async_copy(cv_hbm.at[pl.ds(0, ctile)], cv.at[rs], sem_v.at[b]).wait()
        heads_of = lambda ref: jnp.concatenate([ref[rs, h * 128:(h + 1) * 128] for h in range(heads)], axis=0)
        rep = lambda x: jnp.concatenate([x] * heads, axis=0)
        qt = heads_of(qs)
        kt = ck[rs].reshape(ctile * 128, 128)
        vt = cv[rs].reshape(ctile * 128, 128)
        s = lax.dot_general(qt, kt, NT, preferred_element_type=F32)
        sc = s[:, :128]
        for r in range(1, ctile):
            sc = jnp.where(mrow == r, s[:, r * 128:(r + 1) * 128], sc)
        sc = jnp.where(lane < rep(lens[rs]), sc, NEG)
        so = jnp.sum(qt.astype(F32) * rep(nks[rs]), axis=1, keepdims=True)
        mp = heads_of(mbuf)
        m = jnp.maximum(jnp.maximum(mp, jnp.max(sc, axis=1, keepdims=True)), so)
        ap = jnp.exp2((mp - m) * SCALE2)
        e = jnp.exp2((sc - m) * SCALE2)
        eo = jnp.exp2((so - m) * SCALE2)
        eb = e.astype(BF).astype(F32)
        pe = jnp.concatenate([jnp.where(mrow == r, eb, 0.0).astype(BF) for r in range(ctile)], axis=1)
        oc = jnp.dot(pe, vt, preferred_element_type=F32)
        l = ap * heads_of(lbuf) + jnp.sum(e, axis=1, keepdims=True) + eo
        o = (ap * heads_of(acc) + oc + eo * rep(nvs[rs])) / l
        for h in range(heads):
            qs[rs, h * 128:(h + 1) * 128] = o[h * ctile:(h + 1) * ctile].astype(BF)
        return 0

    lax.fori_loop(0, ctiles, cached, 0)
    out_ref[...] = jnp.dot(unperm, qs[...], preferred_element_type=F32).astype(BF)


def attend(queries, new_key, new_value, ck, cv, lengths, pk, pv, prompt_ids, tile=32):
    rows = queries.shape[0]
    width = queries.shape[1]
    keys = pk.shape[2]
    heads = width // 128
    V = pl.BlockSpec(memory_space=pltpu.VMEM)
    A = pl.BlockSpec(memory_space=pl.ANY)
    S = pl.BlockSpec(memory_space=pltpu.SMEM)
    return pl.pallas_call(
        functools.partial(attn_kernel, rows, tile),
        out_shape=jax.ShapeDtypeStruct((rows, width), BF),
        in_specs=[A] * 10,
        out_specs=V,
        scratch_shapes=[
            pltpu.SMEM((rows,), jnp.int32), pltpu.VMEM((1, rows), jnp.int32), pltpu.VMEM((1, rows), jnp.int32),
            pltpu.VMEM((rows, width), BF), pltpu.VMEM((rows, 128), BF), pltpu.VMEM((rows, 128), BF),
            pltpu.VMEM((2, keys, 128), BF), pltpu.VMEM((2, keys, 128), BF),
            pltpu.VMEM((rows, 128, 128), BF), pltpu.VMEM((rows, 128, 128), BF),
            pltpu.VMEM((rows, width), BF), pltpu.VMEM((rows, 128), F32), pltpu.VMEM((rows, 128), F32),
            pltpu.VMEM((rows, 128), F32),
            pltpu.VMEM((rows, width), F32), pltpu.VMEM((rows, width), F32), pltpu.VMEM((rows, width), F32),
            pltpu.VMEM((heads * tile, keys), F32),
            pltpu.SemaphoreType.DMA((6,)), pltpu.SemaphoreType.DMA((2, 2)), pltpu.SemaphoreType.DMA((rows // 16,)), pltpu.SemaphoreType.DMA((rows // 16,)),
        ],
        compiler_params=pltpu.CompilerParams(vmem_limit_bytes=LIMIT),
        cost_estimate=pl.CostEstimate(flops=16 * 10**9, bytes_accessed=11 * 1024 * 1024, transcendentals=2 * 1024 * 1024),
    )(prompt_ids, prompt_ids.reshape(1, rows), lengths.reshape(1, rows), queries, new_key, new_value,
      pk.reshape(2, keys, 128), pv.reshape(2, keys, 128), ck.reshape(rows, 128, 128), cv.reshape(rows, 128, 128))


def swap(x, axis):
    return lax.ppermute(x, axis, [(0, 1), (1, 0)])


def shift(x, by):
    return lax.ppermute(x, "z", [(i, (i + by) % 4) for i in range(4)])


def tiny(mib, flops=1024, **kw):
    return dict(
        compiler_params=pltpu.CompilerParams(vmem_limit_bytes=mib * 1024 * 1024),
        cost_estimate=pl.CostEstimate(flops=flops, bytes_accessed=1024, transcendentals=0),
        **kw,
    )


def hold_kernel(*refs):
    pass


def hold(x, *tokens, mib=4):
    A = pl.BlockSpec(memory_space=pl.ANY)
    return pl.pallas_call(
        hold_kernel,
        out_shape=jax.ShapeDtypeStruct(x.shape, x.dtype),
        in_specs=[A] * (1 + len(tokens)),
        out_specs=A,
        input_output_aliases={0: 0},
        **tiny(mib),
    )(x, *tokens)


def proj_kernel(steps, *refs):
    count = len(steps)
    given = len(refs) - 8 - (count == 1)
    rows, weights = refs[:given], refs[given : given + 4]
    out, w, chunks, sems = refs[-4:]
    loads = [
        pltpu.make_async_copy(src, w.at[:, j * 512 : (j + 1) * 512], sems.at[j])
        for j, src in enumerate(weights)
    ]
    for load in loads:
        load.start()
    a = jnp.concatenate([row[...] for row in rows], axis=0)
    z = lax.axis_index("z")
    xh = lax.axis_index("xh")
    leave = []
    for j in range(4):
        loads[j].wait()
        total = jnp.dot(a, w[:, j * 512 : (j + 1) * 512], preferred_element_type=F32).astype(BF)
        total = total.reshape(count, 2, 64, 512)
        for i in range(count):
            chunks[j // 2, i, :, :, (j % 2) * 512 : (j % 2 + 1) * 512] = total[i]
        if j % 2:
            for i, step in enumerate(steps):
                first = ((xh ^ (j // 2)) * 4 + ((z - step) & 3)) * 2
                leave.append(
                    pltpu.make_async_copy(chunks.at[j // 2, i], out.at[pl.ds(first, 2)], sems.at[4 + j // 2 * count + i])
                )
                leave[-1].start()
    for copy in leave:
        copy.wait()


def project(steps, *ins):
    count = len(steps)
    more = count == 1
    given = len(ins) - 4 - more
    V = pl.BlockSpec(memory_space=pltpu.VMEM)
    A = pl.BlockSpec(memory_space=pl.ANY)
    return pl.pallas_call(
        functools.partial(proj_kernel, steps),
        out_shape=jax.ShapeDtypeStruct((16, 64, 1024), BF),
        in_specs=[V] * given + [A] * (len(ins) - given),
        out_specs=A,
        input_output_aliases={given + 4: 0} if more else {},
        scratch_shapes=[
            pltpu.VMEM((1024, 2048), BF),
            pltpu.VMEM((2, count, 2, 64, 1024), BF),
            pltpu.SemaphoreType.DMA((4 + 2 * count,)),
        ],
        **tiny(48, 0),
    )(*ins)


def up_kernel(
    parts, res, extra, res_y, gain, gain_par, up_mine, up_par,
    hm_ref, hp_ref, sent_ref, res_v, gain_v, gain2_v, w, sent, sems,
):
    c = lax.axis_index("c")
    yl = lax.axis_index("yl")
    here = pl.ds(pl.multiple_of(yl * 64, 64), 64)
    there = pl.ds(pl.multiple_of(64 - yl * 64, 64), 64)
    small = [
        pltpu.make_async_copy(src, dst, sems.at[i // 4, i % 4])
        for i, (src, dst) in enumerate((
            (res.at[pl.ds(pl.multiple_of(c * 128 + yl * 64, 64), 64)], res_v.at[here, :512]),
            (extra.at[here], res_v.at[here, 512:]),
            (res_y, res_v.at[there]),
            (gain, gain_v), (gain_par, gain2_v),
        ))
    ]
    loads = []
    for j in range(4):
        cols = slice(j * 1024, (j + 1) * 1024)
        loads.append((
            pltpu.make_async_copy(up_mine.at[:, cols], w.at[0:512, cols], sems.at[2, j]),
            pltpu.make_async_copy(up_par.at[:, cols], w.at[512:1024, cols], sems.at[3, j]),
        ))
        for load in loads[-1]:
            load.start()
        if j == 0:
            for copy in small:
                copy.start()
    for copy in small:
        copy.wait()

    def summed(first):
        total = parts[first].astype(F32)
        for i in range(1, 8):
            total = total + parts[first + i].astype(F32)
        return total

    mixed = jnp.concatenate([summed(0), summed(8)], axis=0)
    hid = (res_v[...].astype(F32) + mixed).astype(BF)
    hm_ref[...] = hid[:, :512]
    hp_ref[...] = hid[:, 512:]
    wide = hid.astype(F32)
    squares = jnp.sum(wide * wide, axis=1, keepdims=True)
    hi = squares.astype(BF).astype(F32)
    lane = lax.broadcasted_iota(jnp.int32, (128, 128), 1)
    sent[:, 4096:] = jnp.where(lane == 0, hi, jnp.where(lane == 1, squares - hi, 0.0)).astype(BF)
    gains = jnp.concatenate([gain_v[0:1], gain2_v[0:1]], axis=1).astype(F32)
    gained = (wide * gains).astype(BF)
    leave = []
    for j in range(4):
        cols = slice(j * 1024, (j + 1) * 1024)
        for load in loads[j]:
            load.wait()
        sent[:, cols] = jnp.dot(gained, w[:, cols], preferred_element_type=F32).astype(BF)
        out = slice(j * 1024, (j + 1) * 1024 + (128 if j == 3 else 0))
        leave.append(pltpu.make_async_copy(sent.at[:, out], sent_ref.at[:, out], sems.at[4, j]))
        leave[-1].start()
    for copy in leave:
        copy.wait()


def verify_up(*ins):
    V = pl.BlockSpec(memory_space=pltpu.VMEM)
    A = pl.BlockSpec(memory_space=pl.ANY)
    return pl.pallas_call(
        up_kernel,
        out_shape=(
            jax.ShapeDtypeStruct((128, 512), BF),
            jax.ShapeDtypeStruct((128, 512), BF),
            jax.ShapeDtypeStruct((128, 4096 + 128), BF),
        ),
        in_specs=[V] + [A] * 7,
        out_specs=(V, V, A),
        scratch_shapes=[
            pltpu.VMEM((128, 1024), BF),
            pltpu.VMEM((16, 512), BF),
            pltpu.VMEM((16, 512), BF),
            pltpu.VMEM((1024, 4096), BF),
            pltpu.VMEM((128, 4096 + 128), BF),
            pltpu.SemaphoreType.DMA((5, 4)),
        ],
        **tiny(48),
    )(*ins)


def score_kernel(got_hbm, head_hbm, prompts_hbm, clusters_hbm, out_ref, got, head, prompts, clusters, sems):
    copies = [
        pltpu.make_async_copy(src, dst, sems.at[i])
        for i, (src, dst) in enumerate((
            (got_hbm, got), (head_hbm, head), (prompts_hbm, prompts), (clusters_hbm, clusters)
        ))
    ]
    for copy in copies:
        copy.start()
    for copy in copies:
        copy.wait()

    def summed(cols):
        total = got[0, :, cols].astype(F32)
        for i in range(1, 8):
            total = total + got[i, :, cols].astype(F32)
        return total

    tail = summed(slice(4096, 4224))
    squares = tail[:, 0:1] + tail[:, 1:2]
    factor = lax.rsqrt(squares / D + eps)
    acc = jnp.zeros((16, 512), F32)
    for j in range(0, 4096, 512):
        cols = slice(j, j + 512)
        up = summed(cols) * factor
        acc = acc + up / (1.0 + jnp.exp(-up)) * head[0:1, cols]
    scores = jnp.sum(acc, axis=1, keepdims=True)
    row = lax.broadcasted_iota(jnp.int32, (16, 128), 0)
    lane = lax.broadcasted_iota(jnp.int32, (16, 128), 1)
    line = jnp.sum(jnp.where(row == lane, scores, 0.0), axis=0, keepdims=True)
    pair = ((prompts[...] & 1) * CLUSTERS + clusters[...]).astype(F32)
    t = lax.axis_index(TP)
    pair = pltpu.roll(jnp.broadcast_to(pair, (8, 128)), (144 - t * 16) & 127, 1)[0:1]
    lane = lane[0:1]
    mine = jnp.where(lane < 16, line, jnp.where(lane < 32, pair, 0.0))
    out_ref[...] = jnp.broadcast_to(mine.reshape(1, 1, 128), (128, 1, 128))


def score(got, head_weight, prompt_ids, cluster_ids):
    V = pl.BlockSpec(memory_space=pltpu.VMEM)
    A = pl.BlockSpec(memory_space=pl.ANY)
    return pl.pallas_call(
        score_kernel,
        out_shape=jax.ShapeDtypeStruct((128, 1, 128), F32),
        in_specs=[A] * 4,
        out_specs=V,
        scratch_shapes=[
            pltpu.VMEM((8, 16, 4096 + 128), BF),
            pltpu.VMEM((1, 4096), F32),
            pltpu.VMEM((1, 128), jnp.int32),
            pltpu.VMEM((1, 128), jnp.int32),
            pltpu.SemaphoreType.DMA((4,)),
        ],
        **tiny(40),
    )(got, head_weight.astype(F32).reshape(1, 4096), prompt_ids.reshape(1, 128), cluster_ids.reshape(1, 128))


def vote_kernel(all_hbm, scores_ref, votes_ref, x3, x, vals, ids, votes, sem):
    copy = pltpu.make_async_copy(all_hbm, x3, sem)
    copy.start()
    copy.wait()
    x[...] = x3[...].reshape(128, 128)
    t = lax.axis_index(TP)
    lane8 = lax.broadcasted_iota(jnp.int32, (8, 128), 1)
    row8 = lax.broadcasted_iota(jnp.int32, (8, 128), 0)
    lane = lax.broadcasted_iota(jnp.int32, (16, 128), 1)
    place = lane8 // 16 == row8

    def line(block, first):
        front = pltpu.roll(block, 128 - first, 1) if first else block
        rolled = pltpu.roll(front, 0, 1, stride=16, stride_axis=0)
        return jnp.sum(jnp.where(place, rolled, 0.0), axis=0, keepdims=True)

    def scores_of(zx, c):
        base = (zx & 1) * 64 + c * 8 + (zx >> 1) * 2
        return jnp.concatenate(
            [x[pl.ds(base, 4, stride=16), :], x[pl.ds(base + 1, 4, stride=16), :]], axis=0
        )

    for c in range(2):
        scores_ref[c : c + 1, :] = line(scores_of(t, c), 0)
    for zx in range(8):
        for c in range(2):
            dp = zx * 2 + c
            vals[dp : dp + 1, :] = line(scores_of(zx, c), 0)
            ids[dp : dp + 1, :] = line(x[dp * 8 : dp * 8 + 8, :], 16)
    votes[...] = jnp.zeros((128, 128), F32)
    for p in range(2):
        acc = jnp.zeros((16, 128), F32)
        for k in range(CLUSTERS):
            hit = jnp.where(ids[...] == float(p * CLUSTERS + k), vals[...], 0.0)
            acc = jnp.where(lane == k, jnp.sum(hit, axis=1, keepdims=True), acc)
        votes[pl.ds(p, 16, stride=2), :] = acc
    votes_ref[...] = votes[...].T[:CLUSTERS, :32]


def tally(everyone):
    V = pl.BlockSpec(memory_space=pltpu.VMEM)
    A = pl.BlockSpec(memory_space=pl.ANY)
    return pl.pallas_call(
        vote_kernel,
        out_shape=(jax.ShapeDtypeStruct((2, 128), F32), jax.ShapeDtypeStruct((CLUSTERS, 32), F32)),
        in_specs=[A],
        out_specs=(V, V),
        scratch_shapes=[
            pltpu.VMEM((128, 1, 128), F32),
            pltpu.VMEM((128, 128), F32),
            pltpu.VMEM((16, 128), F32),
            pltpu.VMEM((16, 128), F32),
            pltpu.VMEM((128, 128), F32),
            pltpu.SemaphoreType.DMA,
        ],
        **tiny(40),
    )(everyone)


def body(
    queries,
    new_key,
    new_value,
    cache_keys,
    cache_values,
    lengths,
    prefix_keys,
    prefix_values,
    prompt_ids,
    cluster_ids,
    out_weight,
    residual,
    norm_gain,
    up_weight,
    head_weight,
):
    c = lax.axis_index("c")
    yl = lax.axis_index("yl")

    def rows_of(x, first, count):
        return lax.dynamic_slice_in_dim(x, first, count, 0)

    w10 = swap(out_weight, "xh")
    up_par = swap(up_weight, "c")
    w01 = swap(out_weight, "c")

    part = attend(
        queries,
        new_key,
        new_value,
        cache_keys,
        cache_values,
        lengths,
        prefix_keys,
        prefix_values,
        prompt_ids,
    )

    part = hold(part, up_par, w01, mib=63)
    before, after = shift(part, 1), shift(part, 3)
    far = (shift(before[:64], 1), shift(after[64:], 3))
    later = hold(residual, part)
    gain = norm_gain[None, :] + later[:16] * 0
    gain_par = swap(gain, "c")
    extra = swap(rows_of(later, (1 - c) * 128, 128), "c")
    res_y = swap(
        jnp.concatenate(
            [rows_of(later, c * 128 + (1 - yl) * 64, 64), rows_of(extra, (1 - yl) * 64, 64)], axis=1
        ),
        "yl",
    )
    w10 = hold(w10, before, after, res_y, gain_par)
    w11 = swap(w10, "c")

    weights = (out_weight, w01, w10, w11)
    partial = project((0, 1, 3), part, before, after, *weights)
    partial = project((2,), *far, *weights, partial)
    parts = lax.all_to_all(partial, ("xh", "xl", "yh", "yl"), 0, 0, tiled=True)
    hid_mine, hid_par, sent = verify_up(parts, residual, extra, res_y, gain, gain_par, up_weight, up_par)
    got = lax.all_to_all(sent.reshape(8, 16, 4096 + 128), ("z", "xh"), 0, 0, tiled=True)

    hid_back = swap(hid_par, "c")
    away = jnp.concatenate([rows_of(hid_mine, (1 - yl) * 64, 64), rows_of(hid_back, (1 - yl) * 64, 64)], axis=1)
    home = jnp.concatenate([rows_of(hid_mine, yl * 64, 64), rows_of(hid_back, yl * 64, 64)], axis=1)
    came = swap(away, "yl")
    block = jnp.where(
        yl == 0, jnp.concatenate([home, came], axis=0), jnp.concatenate([came, home], axis=0)
    )
    mine, back = block[:, :512], block[:, 512:]
    hidden = jnp.where(
        c == 0, jnp.concatenate([mine, back], axis=0), jnp.concatenate([back, mine], axis=0)
    )

    line = score(got, head_weight, prompt_ids, cluster_ids)
    scores, votes = tally(lax.all_to_all(line, AXES, 0, 0, tiled=True))
    return hidden, scores.reshape(256), votes.T


def solution(mesh):
    fine = Mesh(mesh.devices.reshape(4, 2, 2, 2, 2, 2), AXES)
    placed = (
        P(DP, TP),
        P(DP, TP),
        P(DP, TP),
        P(DP, TP, None, None),
        P(DP, TP, None, None),
        P(DP),
        P(DP, TP, None, None),
        P(DP, TP, None, None),
        P(DP),
        P(DP),
        P(TP, DP),
        P(TP, DP),
        P(DP),
        P(DP, None),
        P(),
    )
    return jax.shard_map(
        body,
        mesh=fine,
        in_specs=placed,
        out_specs=(P(TP, DP), P(TP), P()),
        check_vma=False,
    )
```
